256 devices in a mesh: traj: 8 (over y, core), feat: 32 (over z, x).
Axes of the slice: x: 4, y: 4, z: 8, core: 2. Of those that a mesh axis runs over, the one named last changes fastest.
Arguments:
- frames_now: bfloat16 [4096, 131072], P('traj', 'feat'), may hold values from -6 to 6
- frames_lag: bfloat16 [4096, 131072], P('traj', 'feat'), may hold values from -6 to 6
- test_matrix: bfloat16 [131072, 256], P('feat'), may hold values from -0.015625 to 0.015625
- feature_scale: float32 [131072], P('feat'), may hold values from 0.1 to 8
Outputs:
- basis: bfloat16 [131072, 256], P('feat')
- upper: float32 [256, 256], replicated
The draws below stay inside these ranges and needn't reach their ends.
All inputs are finite; a program needn't handle non-finite values.
Results may differ from the reference program's by a relative error of at most 0.006.
Values may be sent and summed in bfloat16 or wider, within the bound.
No kernel may reach another device: no remote copies, remote signals or barrier semaphores. Data moves between devices by JAX's collectives and lax.ppermute only.
A program may use at most 64 MiB of HBM per device.

```python
import jax
import jax.numpy as jnp
from jax import lax

K = 256
FRAMES = 4096
F = 131072


def draw_feature_scale(key, part):
    position = jnp.arange(F, dtype=jnp.float32) / F
    rising = jnp.exp(position * jnp.log(3.0))
    rough = jnp.exp(jax.random.uniform(key, (F,), jnp.float32, -0.8, 0.8))
    return (rising * rough).astype(jnp.float32)


def steps_of(rng, shape, shards, low, largest):
    level = 1.0
    for dim, shards_of in shards:
        steps = jax.random.uniform(jax.random.fold_in(jax.random.fold_in(rng, 6), dim), (shards_of,), jnp.float32, low / len(shards), largest / len(shards))
        level = level * jnp.repeat(jnp.exp(steps), shape[dim] // shards_of).reshape((-1,) + (1,) * (len(shape) - 1 - dim))
    return level


def scatter_about(rng, extent, width, most, split=(), held_as=jnp.bfloat16):
    entries = jax.random.normal(rng, extent, jnp.float32) * width
    if len(split) > 0:
        entries = steps_of(rng, extent, split, -0.22, 0.18) * entries
    return jnp.clip(entries, min=-most, max=most).astype(held_as)


def setup_inputs(seed: int = 0) -> dict:
    keys = jax.random.split(jax.random.key(seed), 5)
    return {
        "frames_now": scatter_about(keys[0], (FRAMES, F), 1.0, 6.0, ((0, 8), (1, 32))),
        "frames_lag": scatter_about(keys[1], (FRAMES, F), 1.0, 6.0, ((0, 8), (1, 32))),
        "test_matrix": scatter_about(keys[2], (F, K), F ** -0.5, 0.015625, ((0, 32),)),
        "feature_scale": draw_feature_scale(jax.random.fold_in(keys[4], 71), 0),
    }


def reference(frames_now, frames_lag, test_matrix, feature_scale):
    scaled_test = (feature_scale[:, None] * test_matrix.astype(jnp.float32)).astype(jnp.bfloat16)
    proj_now = jnp.dot(frames_now.astype(jnp.float32), scaled_test.astype(jnp.float32), preferred_element_type=jnp.float32).astype(jnp.bfloat16)
    proj_lag = jnp.dot(frames_lag.astype(jnp.float32), scaled_test.astype(jnp.float32), preferred_element_type=jnp.float32).astype(jnp.bfloat16)
    contract = (((0,), (0,)), ((), ()))
    cross = lax.dot_general(frames_now.astype(jnp.float32), proj_lag.astype(jnp.float32), contract, preferred_element_type=jnp.float32)
    cross = cross + lax.dot_general(frames_lag.astype(jnp.float32), proj_now.astype(jnp.float32), contract, preferred_element_type=jnp.float32)
    sketch = feature_scale[:, None] * (0.5 / FRAMES) * cross
    gram = jnp.dot(sketch.T.astype(jnp.float32), sketch.astype(jnp.float32), precision=lax.Precision.HIGHEST, preferred_element_type=jnp.float32)
    lower = jnp.linalg.cholesky(gram)
    solved = lax.linalg.triangular_solve(lower, sketch, left_side=False, lower=True, transpose_a=True)
    basis = (solved * jnp.sqrt(jnp.float32(F))).astype(jnp.bfloat16)
    return (basis, lower.T)
```

```python
import jax
import jax.numpy as jnp
from jax import lax
from jax.experimental import pallas as pl
from jax.experimental.pallas import tpu as pltpu
from jax.sharding import Mesh
from jax.sharding import PartitionSpec as P

F32 = jnp.float32
BF16 = jnp.bfloat16
EXACT = lax.Precision.HIGHEST


def shifted(x, axis, by):
    n = lax.axis_size(axis)
    return lax.ppermute(x, axis, [((i + by) % n, i) for i in range(n)])


def swapped(x, axis, mask):
    n = lax.axis_size(axis)
    return lax.ppermute(x, axis, [(i ^ mask, i) for i in range(n)])


def piece(x, index, size):
    return lax.dynamic_slice_in_dim(x, index * size, size, axis=0)


def scatter_sum(x, axis):
    n = lax.axis_size(axis)
    me = lax.axis_index(axis)
    size = x.shape[0] // n
    total = piece(x, me, size).astype(F32)
    for by in (2, 1, 3) if n == 4 else (1,):
        total = total + shifted(piece(x, (me + by) % n, size), axis, n - by).astype(F32)
    return total


def gather(x, axis):
    n = lax.axis_size(axis)
    me = lax.axis_index(axis)
    size = x.shape[0]
    out = jnp.zeros((n * size, x.shape[1]), x.dtype)
    out = lax.dynamic_update_slice_in_dim(out, x, me * size, axis=0)
    for by in (2, 1, 3) if n == 4 else (1,):
        out = lax.dynamic_update_slice_in_dim(out, shifted(x, axis, by), ((me + by) % n) * size, axis=0)
    return out


def ring_sum(x, axis):
    own = x.astype(BF16)
    before = shifted(own, axis, -1).astype(F32)
    after = shifted(own, axis, 1).astype(F32)
    two = x + before
    three = two + after
    far = shifted(three.astype(BF16), axis, 3).astype(F32)
    near = shifted(two.astype(BF16), axis, -2).astype(F32)
    return three + (far + near)


def exact_sum(x, axis):
    if lax.axis_size(axis) == 4:
        return (x + swapped(x, axis, 1)) + (swapped(x, axis, 2) + swapped(x, axis, 3))
    x = (x + swapped(x, axis, 1)) + (swapped(x, axis, 6) + swapped(x, axis, 7))
    return x + swapped(x, axis, 2)


def factor_block(tile, lead, size):
    groups = size // 8
    rows = [tile[8 * g : 8 * g + 8, :] for g in range(groups)]
    sub = lax.broadcasted_iota(jnp.int32, (8, 128), 0)
    for q in range(groups):
        first = lead + 8 * q
        column = [
            [jnp.broadcast_to(rows[g][:, first + k : first + k + 1], (8, 128)) for g in range(q, groups)]
            for k in range(8)
        ]
        pivots = jnp.zeros((8, 128), F32)
        for j in range(8):
            pivot = jnp.broadcast_to(column[j][0][j : j + 1, :], (8, 128))
            inverse = 1.0 / pivot
            pivots = jnp.where(sub == j, pivot, pivots)
            factor = [c * inverse for c in column[j]]
            factor[0] = jnp.where(sub > j, factor[0], 0.0)
            for k in range(j + 1, 8):
                top = jnp.broadcast_to(column[k][0][j : j + 1, :], (8, 128))
                column[k] = [c - f * top for c, f in zip(column[k], factor)]
            top = jnp.broadcast_to(rows[q][j : j + 1, :], (8, 128))
            for g in range(q, groups):
                rows[g] = rows[g] - factor[g - q] * top
        rows[q] = rows[q] * lax.rsqrt(pivots)
    return jnp.concatenate(rows, axis=0)


def factor_kernel(scale, gram_ref, upper_ref, high_ref, low_ref, work):
    n = gram_ref.shape[0]
    size = 64
    row = lax.broadcasted_iota(jnp.int32, (n, n), 0)
    col = lax.broadcasted_iota(jnp.int32, (n, n), 1)
    work[:, :n] = gram_ref[...]
    work[:, n:] = jnp.where(row == col, 1.0, 0.0).astype(F32)
    block_row = lax.broadcasted_iota(jnp.int32, (size, 128), 0)
    block_col = lax.broadcasted_iota(jnp.int32, (size, 128), 1)
    for r0 in range(0, n, size):
        r1 = r0 + size
        lead = r0 % 128
        other = (lead + size) % 128
        tile = work[r0:r1, r0 - lead : r0 - lead + 128]
        mine = (block_col >= lead) & (block_col < lead + size)
        tile = jnp.where(mine, tile, jnp.where(block_col - other == block_row, 1.0, 0.0))
        tile = factor_block(tile, lead, size)
        inverse = tile[:, other : other + size]
        panel = jnp.dot(inverse, work[r0:r1, :], precision=EXACT, preferred_element_type=F32)
        work[r0:r1, :] = panel
        if r1 < n:
            work[r1:, :] = work[r1:, :] - lax.dot_general(
                panel[:, r1:n], panel, (((0,), (0,)), ((), ())), precision=EXACT, preferred_element_type=F32
            )
    upper_ref[...] = jnp.where(row <= col, work[:, :n], 0.0)
    inverse = jnp.where(row >= col, work[:, n:], 0.0) * scale
    high = inverse.astype(BF16)
    high_ref[...] = high
    low_ref[...] = (inverse - high.astype(F32)).astype(BF16)


def factorize(gram, scale):
    n = gram.shape[0]
    whole = pl.BlockSpec(memory_space=pltpu.VMEM)
    return pl.pallas_call(
        lambda *refs: factor_kernel(scale, *refs),
        out_shape=[
            jax.ShapeDtypeStruct((n, n), F32),
            jax.ShapeDtypeStruct((n, n), BF16),
            jax.ShapeDtypeStruct((n, n), BF16),
        ],
        in_specs=[whole],
        out_specs=[whole] * 3,
        scratch_shapes=[pltpu.VMEM((n, 2 * n), F32)],
        compiler_params=pltpu.CompilerParams(vmem_limit_bytes=16 * 2**20),
        cost_estimate=pl.CostEstimate(flops=12 * n * n * n, bytes_accessed=8 * n * n, transcendentals=0),
        name="factorize",
    )(gram)


def on_device(frames_now, frames_lag, test_matrix, feature_scale):
    frames, features = frames_now.shape
    frame_total = frames * lax.axis_size(("y", "c"))
    feature_total = features * lax.axis_size(("z", "x"))
    scaled_test = (feature_scale[:, None] * test_matrix.astype(F32)).astype(BF16)
    part_now = jnp.dot(frames_now, scaled_test, preferred_element_type=F32)
    part_lag = jnp.dot(frames_lag, scaled_test, preferred_element_type=F32)
    part = jnp.concatenate([part_now.astype(BF16), part_lag.astype(BF16)], axis=0)
    with jax.named_scope("project"):
        proj = gather(ring_sum(scatter_sum(part, "x"), "z").astype(BF16), "x")
    proj_now, proj_lag = proj[:frames], proj[frames:]

    contract = (((0,), (0,)), ((), ()))
    factor = (0.5 / frame_total) * feature_scale
    cross = lax.dot_general(frames_now, proj_lag, contract, preferred_element_type=F32)
    cross = cross + lax.dot_general(frames_lag, proj_now, contract, preferred_element_type=F32)
    cross = (factor[:, None] * cross).astype(BF16)
    with jax.named_scope("sketch"):
        half = scatter_sum(cross, "c")
        sketch = scatter_sum(half.astype(BF16), "y")

    partial = lax.dot_general(sketch, sketch, contract, precision=EXACT, preferred_element_type=F32)
    with jax.named_scope("gram"):
        slab = scatter_sum(scatter_sum(partial, "c"), "y")
        slab = exact_sum(exact_sum(slab, "x"), "z")
        gram = gather(gather(slab, "y"), "c")
    upper, high, low = factorize(gram, feature_total**0.5)
    with jax.named_scope("whole_sketch"):
        whole = gather(gather(sketch.astype(BF16), "y"), "c")
    transposed = (((1,), (1,)), ((), ()))
    basis = lax.dot_general(whole, high, transposed, preferred_element_type=F32)
    basis = basis + lax.dot_general(whole, low, transposed, preferred_element_type=F32)
    return (basis.astype(BF16), upper)


def solution(mesh):
    split = Mesh(mesh.devices.reshape(4, 2, 8, 4), ("y", "c", "z", "x"))
    traj, feat = ("y", "c"), ("z", "x")
    in_specs = (P(traj, feat), P(traj, feat), P(feat, None), P(feat))
    out_specs = (P(feat, None), P())
    return jax.shard_map(
        on_device, mesh=split, in_specs=in_specs, out_specs=out_specs, check_vma=False
    )
```

```python
import jax
import jax.numpy as jnp
from jax import lax
from jax.experimental import pallas as pl
from jax.experimental.pallas import tpu as pltpu
from jax.sharding import Mesh
from jax.sharding import PartitionSpec as P

F32 = jnp.float32
BF16 = jnp.bfloat16
EXACT = lax.Precision.HIGHEST


def shifted(x, axis, by):
    n = lax.axis_size(axis)
    return lax.ppermute(x, axis, [((i + by) % n, i) for i in range(n)])


def swapped(x, axis, mask):
    n = lax.axis_size(axis)
    return lax.ppermute(x, axis, [(i ^ mask, i) for i in range(n)])


def piece(x, index, size):
    return lax.dynamic_slice_in_dim(x, index * size, size, axis=0)


def scatter_sum(x, axis):
    n = lax.axis_size(axis)
    me = lax.axis_index(axis)
    size = x.shape[0] // n
    total = piece(x, me, size).astype(F32)
    for by in (2, 1, 3) if n == 4 else (1,):
        total = total + shifted(piece(x, (me + by) % n, size), axis, n - by).astype(F32)
    return total


def gather(x, axis):
    n = lax.axis_size(axis)
    me = lax.axis_index(axis)
    size = x.shape[0]
    out = jnp.zeros((n * size, x.shape[1]), x.dtype)
    out = lax.dynamic_update_slice_in_dim(out, x, me * size, axis=0)
    for by in (2, 1, 3) if n == 4 else (1,):
        out = lax.dynamic_update_slice_in_dim(out, shifted(x, axis, by), ((me + by) % n) * size, axis=0)
    return out


def ring_sum(x, axis):
    own = x.astype(BF16)
    before = shifted(own, axis, -1).astype(F32)
    after = shifted(own, axis, 1).astype(F32)
    two = x + before
    three = two + after
    far = shifted(three.astype(BF16), axis, 3).astype(F32)
    near = shifted(two.astype(BF16), axis, -2).astype(F32)
    return three + (far + near)


def exact_sum(x, axis):
    if lax.axis_size(axis) == 4:
        return (x + swapped(x, axis, 1)) + (swapped(x, axis, 2) + swapped(x, axis, 3))
    x = (x + swapped(x, axis, 1)) + (swapped(x, axis, 6) + swapped(x, axis, 7))
    return x + swapped(x, axis, 2)


def factor_block(tile, lead, size):
    groups = size // 8
    rows = [tile[8 * g : 8 * g + 8, :] for g in range(groups)]
    sub = lax.broadcasted_iota(jnp.int32, (8, 128), 0)
    for q in range(groups):
        first = lead + 8 * q
        column = [
            [jnp.broadcast_to(rows[g][:, first + k : first + k + 1], (8, 128)) for g in range(q, groups)]
            for k in range(8)
        ]
        pivots = jnp.zeros((8, 128), F32)
        for j in range(8):
            pivot = jnp.broadcast_to(column[j][0][j : j + 1, :], (8, 128))
            inverse = 1.0 / pivot
            pivots = jnp.where(sub == j, pivot, pivots)
            factor = [c * inverse for c in column[j]]
            factor[0] = jnp.where(sub > j, factor[0], 0.0)
            for k in range(j + 1, 8):
                top = jnp.broadcast_to(column[k][0][j : j + 1, :], (8, 128))
                column[k] = [c - f * top for c, f in zip(column[k], factor)]
            top = jnp.broadcast_to(rows[q][j : j + 1, :], (8, 128))
            for g in range(q, groups):
                rows[g] = rows[g] - factor[g - q] * top
        rows[q] = rows[q] * lax.rsqrt(pivots)
    return jnp.concatenate(rows, axis=0)


def factor_kernel(scale, gram_ref, upper_ref, high_ref, low_ref, work):
    n = gram_ref.shape[0]
    size = 64
    row = lax.broadcasted_iota(jnp.int32, (n, n), 0)
    col = lax.broadcasted_iota(jnp.int32, (n, n), 1)
    work[:, :n] = gram_ref[...]
    work[:, n:] = jnp.where(row == col, 1.0, 0.0).astype(F32)
    block_row = lax.broadcasted_iota(jnp.int32, (size, 128), 0)
    block_col = lax.broadcasted_iota(jnp.int32, (size, 128), 1)
    for r0 in range(0, n, size):
        r1 = r0 + size
        lead = r0 % 128
        other = (lead + size) % 128
        tile = work[r0:r1, r0 - lead : r0 - lead + 128]
        mine = (block_col >= lead) & (block_col < lead + size)
        tile = jnp.where(mine, tile, jnp.where(block_col - other == block_row, 1.0, 0.0))
        tile = factor_block(tile, lead, size)
        inverse = tile[:, other : other + size]
        panel = jnp.dot(inverse, work[r0:r1, :], precision=EXACT, preferred_element_type=F32)
        work[r0:r1, :] = panel
        if r1 < n:
            work[r1:, :] = work[r1:, :] - lax.dot_general(
                panel[:, r1:n], panel, (((0,), (0,)), ((), ())), precision=EXACT, preferred_element_type=F32
            )
    upper_ref[...] = jnp.where(row <= col, work[:, :n], 0.0)
    inverse = jnp.where(row >= col, work[:, n:], 0.0) * scale
    high = inverse.astype(BF16)
    high_ref[...] = high
    low_ref[...] = (inverse - high.astype(F32)).astype(BF16)


def factorize(gram, scale):
    n = gram.shape[0]
    whole = pl.BlockSpec(memory_space=pltpu.VMEM)
    return pl.pallas_call(
        lambda *refs: factor_kernel(scale, *refs),
        out_shape=[
            jax.ShapeDtypeStruct((n, n), F32),
            jax.ShapeDtypeStruct((n, n), BF16),
            jax.ShapeDtypeStruct((n, n), BF16),
        ],
        in_specs=[whole],
        out_specs=[whole] * 3,
        scratch_shapes=[pltpu.VMEM((n, 2 * n), F32)],
        compiler_params=pltpu.CompilerParams(vmem_limit_bytes=16 * 2**20),
        cost_estimate=pl.CostEstimate(flops=12 * n * n * n, bytes_accessed=8 * n * n, transcendentals=0),
        name="factorize",
    )(gram)


def project_kernel(now_ref, lag_ref, test_ref, scale_ref, out_ref, acc):
    step = pl.program_id(0)
    frames = now_ref.shape[0]
    columns = test_ref.shape[1]

    @pl.when(step == 0)
    def _():
        acc[...] = jnp.zeros_like(acc)

    scale = jnp.transpose(jnp.broadcast_to(scale_ref[...], (128, scale_ref.shape[1])))
    test = test_ref[...].astype(F32)
    scaled = jnp.concatenate([scale * test[:, i : i + 128] for i in range(0, columns, 128)], axis=1).astype(BF16)
    acc[:frames, :] += jnp.dot(now_ref[...], scaled, preferred_element_type=F32)
    acc[frames:, :] += jnp.dot(lag_ref[...], scaled, preferred_element_type=F32)

    @pl.when(step == pl.num_programs(0) - 1)
    def _():
        out_ref[...] = jnp.transpose(acc[...]).astype(BF16)


def project(frames_now, frames_lag, test_matrix, scale):
    frames, features = frames_now.shape
    columns = test_matrix.shape[1]
    block = 512
    return pl.pallas_call(
        project_kernel,
        grid=(features // block,),
        in_specs=[
            pl.BlockSpec((frames, block), lambda i: (0, i)),
            pl.BlockSpec((frames, block), lambda i: (0, i)),
            pl.BlockSpec((block, columns), lambda i: (i, 0)),
            pl.BlockSpec((1, block), lambda i: (0, i)),
        ],
        out_specs=pl.BlockSpec((columns, 2 * frames), lambda i: (0, 0)),
        out_shape=jax.ShapeDtypeStruct((columns, 2 * frames), BF16),
        scratch_shapes=[pltpu.VMEM((2 * frames, columns), F32)],
        compiler_params=pltpu.CompilerParams(vmem_limit_bytes=60 * 2**20),
        cost_estimate=pl.CostEstimate(
            flops=4 * frames * features * columns, bytes_accessed=4 * frames * features, transcendentals=0
        ),
        name="project",
    )(frames_now, frames_lag, test_matrix, scale)


def cross_kernel(order_ref, proj_ref, now_ref, lag_ref, factor_ref, out_ref):
    del order_ref
    frames = now_ref.shape[0]
    total = jnp.dot(proj_ref[:, frames:], now_ref[...], preferred_element_type=F32)
    total = total + jnp.dot(proj_ref[:, :frames], lag_ref[...], preferred_element_type=F32)
    out_ref[0] = (total * factor_ref[...]).astype(out_ref.dtype)


def cross(order, block, proj, frames_now, frames_lag, factor, dtype):
    frames, features = frames_now.shape
    columns = proj.shape[0]
    count = order.shape[0]
    return pl.pallas_call(
        cross_kernel,
        grid_spec=pltpu.PrefetchScalarGridSpec(
            num_scalar_prefetch=1,
            grid=(count,),
            in_specs=[
                pl.BlockSpec((columns, 2 * frames), lambda i, order: (0, 0)),
                pl.BlockSpec((frames, block), lambda i, order: (0, order[i])),
                pl.BlockSpec((frames, block), lambda i, order: (0, order[i])),
                pl.BlockSpec((1, block), lambda i, order: (0, order[i])),
            ],
            out_specs=pl.BlockSpec((1, columns, block), lambda i, order: (i, 0, 0)),
        ),
        out_shape=jax.ShapeDtypeStruct((count, columns, block), dtype),
        compiler_params=pltpu.CompilerParams(vmem_limit_bytes=50 * 2**20),
        cost_estimate=pl.CostEstimate(
            flops=4 * frames * count * block * columns,
            bytes_accessed=4 * frames * count * block,
            transcendentals=0,
        ),
        name="cross",
    )(order, proj, frames_now, frames_lag, factor)


def combine_kernel(own_ref, came_ref, *out_refs):
    for k, out_ref in enumerate(out_refs):
        out_ref[...] = (own_ref[k + 1] + came_ref[k + 1].astype(F32)).astype(BF16)


def combine(own, came):
    count, columns, block = own.shape
    whole = pl.BlockSpec(memory_space=pltpu.VMEM)
    return pl.pallas_call(
        combine_kernel,
        in_specs=[whole] * 2,
        out_specs=[whole] * (count - 1),
        out_shape=[jax.ShapeDtypeStruct((columns, block), BF16)] * (count - 1),
        compiler_params=pltpu.CompilerParams(vmem_limit_bytes=16 * 2**20),
        name="combine",
    )(own, came)


def gram_kernel(core_ref, own_ref, came_ref, a_ref, b_ref, d_ref, keep_ref, send_ref, rows_ref, work):
    total = own_ref[0] + came_ref[0].astype(F32)
    total = total + (a_ref[...].astype(F32) + b_ref[...].astype(F32) + d_ref[...].astype(F32))
    half = keep_ref.shape[0]
    core = core_ref[0]
    work[...] = lax.dot_general(
        total, total, (((1,), (1,)), ((), ())), precision=EXACT, preferred_element_type=F32
    )
    keep_ref[...] = work[pl.ds(pl.multiple_of(core * half, half), half), :]
    send_ref[...] = work[pl.ds(pl.multiple_of((1 - core) * half, half), half), :]
    rows_ref[...] = jnp.transpose(total).astype(BF16)


def gram_of(core, own, came, others):
    columns, block = own.shape[1:]
    whole = pl.BlockSpec(memory_space=pltpu.VMEM)
    half = jax.ShapeDtypeStruct((columns // 2, columns), F32)
    return pl.pallas_call(
        gram_kernel,
        in_specs=[pl.BlockSpec(memory_space=pltpu.SMEM)] + [whole] * 5,
        out_specs=[whole] * 3,
        out_shape=[half, half, jax.ShapeDtypeStruct((block, columns), BF16)],
        scratch_shapes=[pltpu.VMEM((columns, columns), F32)],
        compiler_params=pltpu.CompilerParams(vmem_limit_bytes=16 * 2**20),
        name="gram",
    )(core, own, came, *others)


def basis_kernel(sketch_ref, high_ref, low_ref, out_ref):
    transposed = (((1,), (1,)), ((), ()))
    total = lax.dot_general(sketch_ref[...], high_ref[...], transposed, preferred_element_type=F32)
    total = total + lax.dot_general(sketch_ref[...], low_ref[...], transposed, preferred_element_type=F32)
    out_ref[...] = total.astype(BF16)


def basis_of(sketch, high, low):
    rows, columns = sketch.shape
    block = 512
    small = pl.BlockSpec((columns, columns), lambda i: (0, 0))
    return pl.pallas_call(
        basis_kernel,
        grid=(rows // block,),
        in_specs=[pl.BlockSpec((block, columns), lambda i: (i, 0)), small, small],
        out_specs=pl.BlockSpec((block, columns), lambda i: (i, 0)),
        out_shape=jax.ShapeDtypeStruct((rows, columns), BF16),
        compiler_params=pltpu.CompilerParams(vmem_limit_bytes=16 * 2**20),
        cost_estimate=pl.CostEstimate(
            flops=4 * rows * columns * columns, bytes_accessed=4 * rows * columns, transcendentals=0
        ),
        name="basis",
    )(sketch, high, low)


def on_device(frames_now, frames_lag, test_matrix, feature_scale):
    frames, features = frames_now.shape
    frame_total = frames * lax.axis_size(("y", "c"))
    feature_total = features * lax.axis_size(("z", "x"))
    ring = lax.axis_size("y")
    scale = feature_scale[None, :]
    factor = (0.5 / frame_total) * scale
    with jax.named_scope("project"):
        part = project(frames_now, frames_lag, test_matrix, scale)
        proj = gather(ring_sum(scatter_sum(part, "x"), "z").astype(BF16), "x")

    with jax.named_scope("sketch"):
        y = lax.axis_index("y")
        c = lax.axis_index("c")
        block = features // (2 * ring)
        turn = (y + jnp.arange(ring, dtype=jnp.int32)) % ring
        sent = cross((1 - c) * ring + turn, block, proj, frames_now, frames_lag, factor, BF16)
        came = swapped(sent, "c", 1)
        own = cross(c * ring + turn, block, proj, frames_now, frames_lag, factor, F32)
        pieces = combine(own, came)
        others = [shifted(pieces[k - 1], "y", -k) for k in (2, 1, 3)]

    with jax.named_scope("gram"):
        keep, send, mine = gram_of(c[None], own, came, others)
        slab = scatter_sum(keep + swapped(send, "c", 1), "y")
        slab, mine = lax.optimization_barrier((slab, mine))
        whole = gather(mine, "y")
        slab = exact_sum(exact_sum(slab, "x"), "z")
        half = gather(slab, "y")
        half, whole = lax.optimization_barrier((half, whole))
        gram = gather(half, "c")
        whole = gather(whole, "c")
        upper, high, low = factorize(gram, feature_total**0.5)
    return (basis_of(whole, high, low), upper)


def solution(mesh):
    split = Mesh(mesh.devices.reshape(4, 2, 8, 4), ("y", "c", "z", "x"))
    traj, feat = ("y", "c"), ("z", "x")
    in_specs = (P(traj, feat), P(traj, feat), P(feat, None), P(feat))
    out_specs = (P(feat, None), P())
    return jax.shard_map(
        on_device, mesh=split, in_specs=in_specs, out_specs=out_specs, check_vma=False
    )
```

```python
import jax
import jax.numpy as jnp
from jax import lax
from jax.experimental import pallas as pl
from jax.experimental.pallas import tpu as pltpu
from jax.sharding import Mesh
from jax.sharding import PartitionSpec as P

F32 = jnp.float32
BF16 = jnp.bfloat16
EXACT = lax.Precision.HIGHEST


def shifted(x, axis, by):
    n = lax.axis_size(axis)
    return lax.ppermute(x, axis, [((i + by) % n, i) for i in range(n)])


def swapped(x, axis, mask):
    n = lax.axis_size(axis)
    return lax.ppermute(x, axis, [(i ^ mask, i) for i in range(n)])


def piece(x, index, size):
    return lax.dynamic_slice_in_dim(x, index * size, size, axis=0)


def scatter_sum(x, axis):
    n = lax.axis_size(axis)
    me = lax.axis_index(axis)
    size = x.shape[0] // n
    total = piece(x, me, size).astype(F32)
    for by in (2, 1, 3) if n == 4 else (1,):
        total = total + shifted(piece(x, (me + by) % n, size), axis, n - by).astype(F32)
    return total


def gather(x, axis):
    n = lax.axis_size(axis)
    me = lax.axis_index(axis)
    size = x.shape[0]
    out = jnp.zeros((n * size, x.shape[1]), x.dtype)
    out = lax.dynamic_update_slice_in_dim(out, x, me * size, axis=0)
    for by in (2, 1, 3) if n == 4 else (1,):
        out = lax.dynamic_update_slice_in_dim(out, shifted(x, axis, by), ((me + by) % n) * size, axis=0)
    return out


def ring_sum(x, axis):
    own = x.astype(BF16)
    before = shifted(own, axis, -1).astype(F32)
    after = shifted(own, axis, 1).astype(F32)
    two = x + before
    three = two + after
    far = shifted(three.astype(BF16), axis, 3).astype(F32)
    near = shifted(two.astype(BF16), axis, -2).astype(F32)
    return three + (far + near)


def exact_sum(x, axis):
    return (x + swapped(x, axis, 1)) + (swapped(x, axis, 2) + swapped(x, axis, 3))


def factor_block(tile, lead, size):
    groups = size // 8
    rows = [tile[8 * g : 8 * g + 8, :] for g in range(groups)]
    sub = lax.broadcasted_iota(jnp.int32, (8, 128), 0)
    for q in range(groups):
        first = lead + 8 * q
        column = [
            [jnp.broadcast_to(rows[g][:, first + k : first + k + 1], (8, 128)) for g in range(q, groups)]
            for k in range(8)
        ]
        pivots = jnp.zeros((8, 128), F32)
        for j in range(8):
            pivot = jnp.broadcast_to(column[j][0][j : j + 1, :], (8, 128))
            inverse = 1.0 / pivot
            pivots = jnp.where(sub == j, pivot, pivots)
            factor = [c * inverse for c in column[j]]
            factor[0] = jnp.where(sub > j, factor[0], 0.0)
            for k in range(j + 1, 8):
                top = jnp.broadcast_to(column[k][0][j : j + 1, :], (8, 128))
                column[k] = [c - f * top for c, f in zip(column[k], factor)]
            top = jnp.broadcast_to(rows[q][j : j + 1, :], (8, 128))
            for g in range(q, groups):
                rows[g] = rows[g] - factor[g - q] * top
        rows[q] = rows[q] * lax.rsqrt(pivots)
    return jnp.concatenate(rows, axis=0)


def factor_kernel(scale, gram_ref, upper_ref, high_ref, low_ref, work):
    n = gram_ref.shape[0]
    size = 64
    row = lax.broadcasted_iota(jnp.int32, (n, n), 0)
    col = lax.broadcasted_iota(jnp.int32, (n, n), 1)
    work[:, :n] = gram_ref[...]
    work[:, n:] = jnp.where(row == col, 1.0, 0.0).astype(F32)
    block_row = lax.broadcasted_iota(jnp.int32, (size, 128), 0)
    block_col = lax.broadcasted_iota(jnp.int32, (size, 128), 1)
    for r0 in range(0, n, size):
        r1 = r0 + size
        lead = r0 % 128
        other = (lead + size) % 128
        tile = work[r0:r1, r0 - lead : r0 - lead + 128]
        mine = (block_col >= lead) & (block_col < lead + size)
        tile = jnp.where(mine, tile, jnp.where(block_col - other == block_row, 1.0, 0.0))
        tile = factor_block(tile, lead, size)
        inverse = tile[:, other : other + size]
        panel = jnp.dot(inverse, work[r0:r1, :], precision=EXACT, preferred_element_type=F32)
        work[r0:r1, :] = panel
        if r1 < n:
            work[r1:, :] = work[r1:, :] - lax.dot_general(
                panel[:, r1:n], panel, (((0,), (0,)), ((), ())), precision=EXACT, preferred_element_type=F32
            )
    upper_ref[...] = jnp.where(row <= col, work[:, :n], 0.0)
    inverse = jnp.where(row >= col, work[:, n:], 0.0) * scale
    high = inverse.astype(BF16)
    high_ref[...] = high
    low_ref[...] = (inverse - high.astype(F32)).astype(BF16)


def factorize(gram, scale):
    n = gram.shape[0]
    whole = pl.BlockSpec(memory_space=pltpu.VMEM)
    return pl.pallas_call(
        lambda *refs: factor_kernel(scale, *refs),
        out_shape=[
            jax.ShapeDtypeStruct((n, n), F32),
            jax.ShapeDtypeStruct((n, n), BF16),
            jax.ShapeDtypeStruct((n, n), BF16),
        ],
        in_specs=[whole],
        out_specs=[whole] * 3,
        scratch_shapes=[pltpu.VMEM((n, 2 * n), F32)],
        compiler_params=pltpu.CompilerParams(vmem_limit_bytes=16 * 2**20),
        cost_estimate=pl.CostEstimate(flops=12 * n * n * n, bytes_accessed=8 * n * n, transcendentals=0),
        name="factorize",
    )(gram)


def in_hbm(x):
    return pltpu.with_memory_space_constraint(x, pltpu.HBM)


def project_kernel(parts, me_ref, now_hbm, lag_hbm, test_hbm, scale_hbm, *refs):
    *piece_refs, frames_both, test, scale_ref, total, sems = refs
    frames, features = now_hbm.shape
    columns = test.shape[1]
    width = features // parts
    copies = []
    scales = pltpu.make_async_copy(scale_hbm, scale_ref, sems.at[3 * parts])
    scales.start()
    for i in range(parts):
        at = pl.ds(i * width, width)
        copies.append(
            [
                pltpu.make_async_copy(test_hbm.at[at], test.at[at], sems.at[3 * i]),
                pltpu.make_async_copy(now_hbm.at[:, at], frames_both.at[pl.ds(0, frames), at], sems.at[3 * i + 1]),
                pltpu.make_async_copy(lag_hbm.at[:, at], frames_both.at[pl.ds(frames, frames), at], sems.at[3 * i + 2]),
            ]
        )
        for copy in copies[-1]:
            copy.start()
    scales.wait()
    for i in range(parts):
        copies[i][0].wait()
        scaled = [
            (jnp.transpose(test[r : r + 128, :]).astype(F32) * scale_ref[:, r : r + 128]).astype(BF16)
            for r in range(i * width, (i + 1) * width, 128)
        ]
        scaled = jnp.concatenate(scaled, axis=1)
        copies[i][1].wait()
        copies[i][2].wait()
        term = lax.dot_general(
            scaled,
            frames_both[:, i * width : (i + 1) * width],
            (((1,), (1,)), ((), ())),
            preferred_element_type=F32,
        )
        total[...] = term if i == 0 else total[...] + term
    count = len(piece_refs)
    size = columns // count
    for k, piece_ref in enumerate(piece_refs):
        at = pl.multiple_of(lax.rem(me_ref[0] + k, count) * size, size)
        piece_ref[...] = total[pl.ds(at, size), :].astype(piece_ref.dtype)


def project(me, count, frames_now, frames_lag, test_matrix, scale):
    frames, features = frames_now.shape
    columns = test_matrix.shape[1]
    parts = 4
    size = columns // count
    vmem = pl.BlockSpec(memory_space=pltpu.VMEM)
    hbm = pl.BlockSpec(memory_space=pl.ANY)
    return pl.pallas_call(
        lambda *refs: project_kernel(parts, *refs),
        in_specs=[pl.BlockSpec(memory_space=pltpu.SMEM), hbm, hbm, hbm, hbm],
        out_specs=[vmem] * count,
        out_shape=[jax.ShapeDtypeStruct((size, 2 * frames), F32)]
        + [jax.ShapeDtypeStruct((size, 2 * frames), BF16)] * (count - 1),
        scratch_shapes=[
            pltpu.VMEM((2 * frames, features), BF16),
            pltpu.VMEM((features, columns), BF16),
            pltpu.VMEM((1, features), F32),
            pltpu.VMEM((columns, 2 * frames), F32),
            pltpu.SemaphoreType.DMA((3 * parts + 1,)),
        ],
        compiler_params=pltpu.CompilerParams(vmem_limit_bytes=32 * 2**20),
        cost_estimate=pl.CostEstimate(
            flops=4 * frames * features * columns, bytes_accessed=4 * frames * features, transcendentals=0
        ),
        name="project",
    )(me[None], in_hbm(frames_now), in_hbm(frames_lag), in_hbm(test_matrix), in_hbm(scale))


def cross_kernel(where_ref, proj_ref, now_hbm, lag_hbm, factor_ref, out_ref, work, sems):
    frames = now_hbm.shape[0]
    count, _, block = out_ref.shape
    copies = []
    for k in range(count):
        first = where_ref[0] * count + lax.rem(where_ref[1] + k, count)
        at = pl.ds(pl.multiple_of(first * block, block), block)
        copies.append(
            [
                pltpu.make_async_copy(now_hbm.at[:, at], work.at[k, pl.ds(0, frames)], sems.at[2 * k]),
                pltpu.make_async_copy(lag_hbm.at[:, at], work.at[k, pl.ds(frames, frames)], sems.at[2 * k + 1]),
            ]
        )
        for copy in copies[-1]:
            copy.start()
    proj = jnp.concatenate([proj_ref[:, frames:], proj_ref[:, :frames]], axis=1)
    for k in range(count):
        for copy in copies[k]:
            copy.wait()
        first = where_ref[0] * count + lax.rem(where_ref[1] + k, count)
        total = jnp.dot(proj, work[k], preferred_element_type=F32)
        factor = factor_ref[:, pl.ds(pl.multiple_of(first * block, block), block)]
        out_ref[k] = (total * factor).astype(out_ref.dtype)


def cross(half, first, count, proj, frames_now, frames_lag, factor, dtype):
    frames, features = frames_now.shape
    columns = proj.shape[0]
    block = features // (2 * count)
    vmem = pl.BlockSpec(memory_space=pltpu.VMEM)
    hbm = pl.BlockSpec(memory_space=pl.ANY)
    return pl.pallas_call(
        cross_kernel,
        in_specs=[pl.BlockSpec(memory_space=pltpu.SMEM), vmem, hbm, hbm, vmem],
        out_specs=vmem,
        out_shape=jax.ShapeDtypeStruct((count, columns, block), dtype),
        scratch_shapes=[
            pltpu.VMEM((count, 2 * frames, block), BF16),
            pltpu.SemaphoreType.DMA((2 * count,)),
        ],
        compiler_params=pltpu.CompilerParams(vmem_limit_bytes=24 * 2**20),
        cost_estimate=pl.CostEstimate(
            flops=2 * frames * features * columns, bytes_accessed=2 * frames * features, transcendentals=0
        ),
        name="cross",
    )(jnp.stack([half, first]), proj, in_hbm(frames_now), in_hbm(frames_lag), factor)


def combine_kernel(own_ref, came_ref, *out_refs):
    for k, out_ref in enumerate(out_refs):
        out_ref[...] = (own_ref[k + 1] + came_ref[k + 1].astype(F32)).astype(BF16)


def combine(own, came):
    count, columns, block = own.shape
    whole = pl.BlockSpec(memory_space=pltpu.VMEM)
    return pl.pallas_call(
        combine_kernel,
        in_specs=[whole] * 2,
        out_specs=[whole] * (count - 1),
        out_shape=[jax.ShapeDtypeStruct((columns, block), BF16)] * (count - 1),
        compiler_params=pltpu.CompilerParams(vmem_limit_bytes=16 * 2**20),
        name="combine",
    )(own, came)


def gram_kernel(core_ref, own_ref, came_ref, a_ref, b_ref, d_ref, keep_ref, send_ref, rows_ref, work):
    total = own_ref[0] + came_ref[0].astype(F32)
    total = total + (a_ref[...].astype(F32) + b_ref[...].astype(F32) + d_ref[...].astype(F32))
    half = keep_ref.shape[0]
    core = core_ref[0]
    work[...] = lax.dot_general(
        total, total, (((1,), (1,)), ((), ())), precision=EXACT, preferred_element_type=F32
    )
    keep_ref[...] = work[pl.ds(pl.multiple_of(core * half, half), half), :]
    send_ref[...] = work[pl.ds(pl.multiple_of((1 - core) * half, half), half), :]
    rows_ref[...] = jnp.transpose(total).astype(BF16)


def gram_of(core, own, came, others):
    columns, block = own.shape[1:]
    whole = pl.BlockSpec(memory_space=pltpu.VMEM)
    half = jax.ShapeDtypeStruct((columns // 2, columns), F32)
    return pl.pallas_call(
        gram_kernel,
        in_specs=[pl.BlockSpec(memory_space=pltpu.SMEM)] + [whole] * 5,
        out_specs=[whole] * 3,
        out_shape=[half, half, jax.ShapeDtypeStruct((block, columns), BF16)],
        scratch_shapes=[pltpu.VMEM((columns, columns), F32)],
        compiler_params=pltpu.CompilerParams(vmem_limit_bytes=16 * 2**20),
        name="gram",
    )(core, own, came, *others)


def basis_kernel(parts, sketch_ref, high_ref, low_ref, out_hbm, work, sems):
    transposed = (((1,), (1,)), ((), ()))
    size = work.shape[0] // parts
    copies = []
    for i in range(parts):
        at = slice(i * size, (i + 1) * size)
        total = lax.dot_general(sketch_ref[at, :], high_ref[...], transposed, preferred_element_type=F32)
        total = total + lax.dot_general(sketch_ref[at, :], low_ref[...], transposed, preferred_element_type=F32)
        work[at, :] = total.astype(BF16)
        rows = pl.ds(i * size, size)
        copies.append(pltpu.make_async_copy(work.at[rows], out_hbm.at[rows], sems.at[i]))
        copies[-1].start()
    for copy in copies:
        copy.wait()


def basis_of(sketch, high, low):
    rows, columns = sketch.shape
    parts = 8
    vmem = pl.BlockSpec(memory_space=pltpu.VMEM)
    return pl.pallas_call(
        lambda *refs: basis_kernel(parts, *refs),
        in_specs=[vmem] * 3,
        out_specs=pl.BlockSpec(memory_space=pl.ANY),
        out_shape=jax.ShapeDtypeStruct((rows, columns), BF16),
        scratch_shapes=[pltpu.VMEM((rows, columns), BF16), pltpu.SemaphoreType.DMA((parts,))],
        compiler_params=pltpu.CompilerParams(vmem_limit_bytes=16 * 2**20),
        cost_estimate=pl.CostEstimate(
            flops=4 * rows * columns * columns, bytes_accessed=4 * rows * columns, transcendentals=0
        ),
        name="basis",
    )(sketch, high, low)


def on_device(frames_now, frames_lag, test_matrix, feature_scale):
    frames, features = frames_now.shape
    frame_total = frames * lax.axis_size(("y", "c"))
    feature_total = features * lax.axis_size(("z", "x"))
    ring = lax.axis_size("y")
    scale = feature_scale[None, :]
    factor = (0.5 / frame_total) * scale
    with jax.named_scope("project"):
        own, *pieces = project(
            lax.axis_index("x"), lax.axis_size("x"), frames_now, frames_lag, test_matrix, scale
        )
        for k in (2, 1, 3):
            own = own + shifted(pieces[k - 1], "x", -k).astype(F32)
        proj = gather(ring_sum(own, "z").astype(BF16), "x")

    with jax.named_scope("sketch"):
        y = lax.axis_index("y")
        c = lax.axis_index("c")
        came = swapped(cross(1 - c, y, ring, proj, frames_now, frames_lag, factor, BF16), "c", 1)
        own = cross(c, y, ring, proj, frames_now, frames_lag, factor, F32)
        pieces = combine(own, came)
        others = [shifted(pieces[k - 1], "y", -k) for k in (2, 1, 3)]

    with jax.named_scope("gram"):
        keep, send, mine = gram_of(c[None], own, came, others)
        slab = scatter_sum(keep + swapped(send, "c", 1), "y")
        slab, mine = lax.optimization_barrier((slab, mine))
        whole = gather(mine, "y")
        slab = exact_sum(slab, "x")
        slab = (slab + swapped(slab, "z", 1)) + (swapped(slab, "z", 6) + swapped(slab, "z", 7))
        slab, whole = lax.optimization_barrier((slab, whole))
        slab = slab + swapped(slab, "z", 2)
        gram = gather(gather(slab, "y"), "c")
        gram, whole = lax.optimization_barrier((gram, whole))
        whole = gather(whole, "c")
        upper, high, low = factorize(gram, feature_total**0.5)
    return (basis_of(whole, high, low), upper)


def solution(mesh):
    split = Mesh(mesh.devices.reshape(4, 2, 8, 4), ("y", "c", "z", "x"))
    traj, feat = ("y", "c"), ("z", "x")
    in_specs = (P(traj, feat), P(traj, feat), P(feat, None), P(feat))
    out_specs = (P(feat, None), P())
    return jax.shard_map(
        on_device, mesh=split, in_specs=in_specs, out_specs=out_specs, check_vma=False
    )
```

```python
import jax
import jax.numpy as jnp
from jax import lax
from jax.experimental import pallas as pl
from jax.experimental.pallas import tpu as pltpu
from jax.sharding import Mesh
from jax.sharding import PartitionSpec as P

F32 = jnp.float32
BF16 = jnp.bfloat16
EXACT = lax.Precision.HIGHEST


def shifted(x, axis, by):
    n = lax.axis_size(axis)
    return lax.ppermute(x, axis, [((i + by) % n, i) for i in range(n)])


def swapped(x, axis, mask):
    n = lax.axis_size(axis)
    return lax.ppermute(x, axis, [(i ^ mask, i) for i in range(n)])


def piece(x, index, size):
    return lax.dynamic_slice_in_dim(x, index * size, size, axis=0)


def scatter_sum(x, axis):
    n = lax.axis_size(axis)
    me = lax.axis_index(axis)
    size = x.shape[0] // n
    total = piece(x, me, size).astype(F32)
    for by in (2, 1, 3) if n == 4 else (1,):
        total = total + shifted(piece(x, (me + by) % n, size), axis, n - by).astype(F32)
    return total


def gather(x, axis):
    n = lax.axis_size(axis)
    me = lax.axis_index(axis)
    size = x.shape[0]
    out = jnp.zeros((n * size, x.shape[1]), x.dtype)
    out = lax.dynamic_update_slice_in_dim(out, x, me * size, axis=0)
    for by in (2, 1, 3) if n == 4 else (1,):
        out = lax.dynamic_update_slice_in_dim(out, shifted(x, axis, by), ((me + by) % n) * size, axis=0)
    return out


def ring_sum(x, axis):
    own = x.astype(BF16)
    before = shifted(own, axis, -1).astype(F32)
    after = shifted(own, axis, 1).astype(F32)
    two = x + before
    three = two + after
    far = shifted(three.astype(BF16), axis, 3).astype(F32)
    near = shifted(two.astype(BF16), axis, -2).astype(F32)
    return three + (far + near)


def exact_sum(x, axis):
    return (x + swapped(x, axis, 1)) + (swapped(x, axis, 2) + swapped(x, axis, 3))


def factor_block(tile, lead, size):
    groups = size // 8
    rows = [tile[8 * g : 8 * g + 8, :] for g in range(groups)]
    sub = lax.broadcasted_iota(jnp.int32, (8, 128), 0)
    for q in range(groups):
        first = lead + 8 * q
        column = [
            [jnp.broadcast_to(rows[g][:, first + k : first + k + 1], (8, 128)) for g in range(q, groups)]
            for k in range(8)
        ]
        pivots = jnp.zeros((8, 128), F32)
        for j in range(8):
            pivot = jnp.broadcast_to(column[j][0][j : j + 1, :], (8, 128))
            inverse = 1.0 / pivot
            pivots = jnp.where(sub == j, pivot, pivots)
            factor = [c * inverse for c in column[j]]
            factor[0] = jnp.where(sub > j, factor[0], 0.0)
            for k in range(j + 1, 8):
                top = jnp.broadcast_to(column[k][0][j : j + 1, :], (8, 128))
                column[k] = [c - f * top for c, f in zip(column[k], factor)]
            top = jnp.broadcast_to(rows[q][j : j + 1, :], (8, 128))
            for g in range(q, groups):
                rows[g] = rows[g] - factor[g - q] * top
        rows[q] = rows[q] * lax.rsqrt(pivots)
    return jnp.concatenate(rows, axis=0)


def factor_kernel(scale, gram_ref, upper_ref, high_ref, low_ref, work):
    n = gram_ref.shape[0]
    size = 64
    row = lax.broadcasted_iota(jnp.int32, (n, n), 0)
    col = lax.broadcasted_iota(jnp.int32, (n, n), 1)
    work[:, :n] = gram_ref[...]
    work[:, n:] = jnp.where(row == col, 1.0, 0.0).astype(F32)
    block_row = lax.broadcasted_iota(jnp.int32, (size, 128), 0)
    block_col = lax.broadcasted_iota(jnp.int32, (size, 128), 1)
    for r0 in range(0, n, size):
        r1 = r0 + size
        lead = r0 % 128
        other = (lead + size) % 128
        tile = work[r0:r1, r0 - lead : r0 - lead + 128]
        mine = (block_col >= lead) & (block_col < lead + size)
        tile = jnp.where(mine, tile, jnp.where(block_col - other == block_row, 1.0, 0.0))
        tile = factor_block(tile, lead, size)
        inverse = tile[:, other : other + size]
        panel = jnp.dot(inverse, work[r0:r1, :], precision=EXACT, preferred_element_type=F32)
        work[r0:r1, :] = panel
        if r1 < n:
            work[r1:, :] = work[r1:, :] - lax.dot_general(
                panel[:, r1:n], panel, (((0,), (0,)), ((), ())), precision=EXACT, preferred_element_type=F32
            )
    upper_ref[...] = jnp.where(row <= col, work[:, :n], 0.0)
    inverse = jnp.where(row >= col, work[:, n:], 0.0) * scale
    high = inverse.astype(BF16)
    high_ref[...] = high
    low_ref[...] = (inverse - high.astype(F32)).astype(BF16)


def factorize(gram, scale):
    n = gram.shape[0]
    whole = pl.BlockSpec(memory_space=pltpu.VMEM)
    return pl.pallas_call(
        lambda *refs: factor_kernel(scale, *refs),
        out_shape=[
            jax.ShapeDtypeStruct((n, n), F32),
            jax.ShapeDtypeStruct((n, n), BF16),
            jax.ShapeDtypeStruct((n, n), BF16),
        ],
        in_specs=[whole],
        out_specs=[whole] * 3,
        scratch_shapes=[pltpu.VMEM((n, 2 * n), F32)],
        compiler_params=pltpu.CompilerParams(vmem_limit_bytes=16 * 2**20),
        cost_estimate=pl.CostEstimate(flops=12 * n * n * n, bytes_accessed=8 * n * n, transcendentals=0),
        name="factorize",
    )(gram)


def in_hbm(x):
    return pltpu.with_memory_space_constraint(x, pltpu.HBM)


def project_kernel(parts, me_ref, now_hbm, lag_hbm, test_hbm, scale_hbm, *refs):
    *piece_refs, frames_both, test, scale_ref, total, sems = refs
    frames, features = now_hbm.shape
    columns = test.shape[1]
    width = features // parts
    copies = []
    scales = pltpu.make_async_copy(scale_hbm, scale_ref, sems.at[3 * parts])
    scales.start()
    for i in range(parts):
        at = pl.ds(i * width, width)
        copies.append(
            [
                pltpu.make_async_copy(test_hbm.at[at], test.at[at], sems.at[3 * i]),
                pltpu.make_async_copy(now_hbm.at[:, at], frames_both.at[pl.ds(0, frames), at], sems.at[3 * i + 1]),
                pltpu.make_async_copy(lag_hbm.at[:, at], frames_both.at[pl.ds(frames, frames), at], sems.at[3 * i + 2]),
            ]
        )
        for copy in copies[-1]:
            copy.start()
    scales.wait()
    for i in range(parts):
        copies[i][0].wait()
        scaled = [
            (jnp.transpose(test[r : r + 128, :]).astype(F32) * scale_ref[:, r : r + 128]).astype(BF16)
            for r in range(i * width, (i + 1) * width, 128)
        ]
        scaled = jnp.concatenate(scaled, axis=1)
        copies[i][1].wait()
        copies[i][2].wait()
        term = lax.dot_general(
            scaled,
            frames_both[:, i * width : (i + 1) * width],
            (((1,), (1,)), ((), ())),
            preferred_element_type=F32,
        )
        total[...] = term if i == 0 else total[...] + term
    count = len(piece_refs)
    size = columns // count
    for k, piece_ref in enumerate(piece_refs):
        at = pl.multiple_of(lax.rem(me_ref[0] + k, count) * size, size)
        piece_ref[...] = total[pl.ds(at, size), :].astype(piece_ref.dtype)


def project(me, count, frames_now, frames_lag, test_matrix, scale):
    frames, features = frames_now.shape
    columns = test_matrix.shape[1]
    parts = 4
    size = columns // count
    vmem = pl.BlockSpec(memory_space=pltpu.VMEM)
    hbm = pl.BlockSpec(memory_space=pl.ANY)
    return pl.pallas_call(
        lambda *refs: project_kernel(parts, *refs),
        in_specs=[pl.BlockSpec(memory_space=pltpu.SMEM), hbm, hbm, hbm, hbm],
        out_specs=[vmem] * count,
        out_shape=[jax.ShapeDtypeStruct((size, 2 * frames), F32)]
        + [jax.ShapeDtypeStruct((size, 2 * frames), BF16)] * (count - 1),
        scratch_shapes=[
            pltpu.VMEM((2 * frames, features), BF16),
            pltpu.VMEM((features, columns), BF16),
            pltpu.VMEM((1, features), F32),
            pltpu.VMEM((columns, 2 * frames), F32),
            pltpu.SemaphoreType.DMA((3 * parts + 1,)),
        ],
        compiler_params=pltpu.CompilerParams(vmem_limit_bytes=32 * 2**20),
        cost_estimate=pl.CostEstimate(
            flops=4 * frames * features * columns, bytes_accessed=4 * frames * features, transcendentals=0
        ),
        name="project",
    )(me[None], in_hbm(frames_now), in_hbm(frames_lag), in_hbm(test_matrix), in_hbm(scale))


def cross_kernel(jobs, where_ref, proj_ref, now_hbm, lag_hbm, factor_ref, *refs):
    *out_refs, work, sems = refs
    frames = now_hbm.shape[0]
    block = out_refs[0].shape[2]
    count = now_hbm.shape[1] // (2 * block)
    places = []
    copies = []
    for n, (_, _, other, slot) in enumerate(jobs):
        half = 1 - where_ref[0] if other else where_ref[0]
        first = half * count + lax.rem(where_ref[1] + slot, count)
        at = pl.ds(pl.multiple_of(first * block, block), block)
        places.append(at)
        copies.append(
            [
                pltpu.make_async_copy(now_hbm.at[:, at], work.at[n, pl.ds(0, frames)], sems.at[2 * n]),
                pltpu.make_async_copy(lag_hbm.at[:, at], work.at[n, pl.ds(frames, frames)], sems.at[2 * n + 1]),
            ]
        )
        for copy in copies[-1]:
            copy.start()
    proj = jnp.concatenate([proj_ref[:, frames:], proj_ref[:, :frames]], axis=1)
    for n, (out, row, _, _) in enumerate(jobs):
        for copy in copies[n]:
            copy.wait()
        total = jnp.dot(proj, work[n], preferred_element_type=F32)
        out_refs[out][row] = (total * factor_ref[:, places[n]]).astype(out_refs[out].dtype)


def cross(core, ring_place, ring, slots_other, slots_own, proj, frames_now, frames_lag, factor):
    frames, features = frames_now.shape
    columns = proj.shape[0]
    block = features // (2 * ring)
    jobs, out_shape = [], []
    for slots, other, dtype in ((slots_other, True, BF16), (slots_own, False, F32)):
        if slots:
            jobs += [(len(out_shape), row, other, slot) for row, slot in enumerate(slots)]
            out_shape.append(jax.ShapeDtypeStruct((len(slots), columns, block), dtype))
    vmem = pl.BlockSpec(memory_space=pltpu.VMEM)
    hbm = pl.BlockSpec(memory_space=pl.ANY)
    return pl.pallas_call(
        lambda *refs: cross_kernel(jobs, *refs),
        in_specs=[pl.BlockSpec(memory_space=pltpu.SMEM), vmem, hbm, hbm, vmem],
        out_specs=[vmem] * len(out_shape),
        out_shape=out_shape,
        scratch_shapes=[
            pltpu.VMEM((len(jobs), 2 * frames, block), BF16),
            pltpu.SemaphoreType.DMA((2 * len(jobs),)),
        ],
        compiler_params=pltpu.CompilerParams(vmem_limit_bytes=24 * 2**20),
        cost_estimate=pl.CostEstimate(
            flops=4 * frames * len(jobs) * block * columns,
            bytes_accessed=4 * frames * len(jobs) * block,
            transcendentals=0,
        ),
        name="cross",
    )(jnp.stack([core, ring_place]), proj, in_hbm(frames_now), in_hbm(frames_lag), factor)


def combine_kernel(own_ref, came_ref, *out_refs):
    for k, out_ref in enumerate(out_refs):
        out_ref[...] = (own_ref[k] + came_ref[k].astype(F32)).astype(BF16)


def combine(own, came, count):
    _, columns, block = own.shape
    whole = pl.BlockSpec(memory_space=pltpu.VMEM)
    return pl.pallas_call(
        combine_kernel,
        in_specs=[whole] * 2,
        out_specs=[whole] * count,
        out_shape=[jax.ShapeDtypeStruct((columns, block), BF16)] * count,
        compiler_params=pltpu.CompilerParams(vmem_limit_bytes=16 * 2**20),
        name="combine",
    )(own, came)


def gram_kernel(core_ref, own_ref, came_ref, a_ref, b_ref, d_ref, keep_ref, send_ref, rows_ref, work):
    total = own_ref[own_ref.shape[0] - 1] + came_ref[own_ref.shape[0] - 1].astype(F32)
    total = total + (a_ref[...].astype(F32) + b_ref[...].astype(F32) + d_ref[...].astype(F32))
    half = keep_ref.shape[0]
    core = core_ref[0]
    work[...] = lax.dot_general(
        total, total, (((1,), (1,)), ((), ())), precision=EXACT, preferred_element_type=F32
    )
    keep_ref[...] = work[pl.ds(pl.multiple_of(core * half, half), half), :]
    send_ref[...] = work[pl.ds(pl.multiple_of((1 - core) * half, half), half), :]
    rows_ref[...] = jnp.transpose(total).astype(BF16)


def gram_of(core, own, came, others):
    columns, block = own.shape[1:]
    whole = pl.BlockSpec(memory_space=pltpu.VMEM)
    half = jax.ShapeDtypeStruct((columns // 2, columns), F32)
    return pl.pallas_call(
        gram_kernel,
        in_specs=[pl.BlockSpec(memory_space=pltpu.SMEM)] + [whole] * 5,
        out_specs=[whole] * 3,
        out_shape=[half, half, jax.ShapeDtypeStruct((block, columns), BF16)],
        scratch_shapes=[pltpu.VMEM((columns, columns), F32)],
        compiler_params=pltpu.CompilerParams(vmem_limit_bytes=16 * 2**20),
        name="gram",
    )(core, own, came, *others)


def basis_kernel(parts, sketch_ref, high_ref, low_ref, out_hbm, work, sems):
    transposed = (((1,), (1,)), ((), ()))
    size = work.shape[0] // parts
    copies = []
    for i in range(parts):
        at = slice(i * size, (i + 1) * size)
        total = lax.dot_general(sketch_ref[at, :], high_ref[...], transposed, preferred_element_type=F32)
        total = total + lax.dot_general(sketch_ref[at, :], low_ref[...], transposed, preferred_element_type=F32)
        work[at, :] = total.astype(BF16)
        rows = pl.ds(i * size, size)
        copies.append(pltpu.make_async_copy(work.at[rows], out_hbm.at[rows], sems.at[i]))
        copies[-1].start()
    for copy in copies:
        copy.wait()


def basis_of(sketch, high, low):
    rows, columns = sketch.shape
    parts = 8
    vmem = pl.BlockSpec(memory_space=pltpu.VMEM)
    return pl.pallas_call(
        lambda *refs: basis_kernel(parts, *refs),
        in_specs=[vmem] * 3,
        out_specs=pl.BlockSpec(memory_space=pl.ANY),
        out_shape=jax.ShapeDtypeStruct((rows, columns), BF16),
        scratch_shapes=[pltpu.VMEM((rows, columns), BF16), pltpu.SemaphoreType.DMA((parts,))],
        compiler_params=pltpu.CompilerParams(vmem_limit_bytes=16 * 2**20),
        cost_estimate=pl.CostEstimate(
            flops=4 * rows * columns * columns, bytes_accessed=4 * rows * columns, transcendentals=0
        ),
        name="basis",
    )(sketch, high, low)


def on_device(frames_now, frames_lag, test_matrix, feature_scale):
    frames, features = frames_now.shape
    frame_total = frames * lax.axis_size(("y", "c"))
    feature_total = features * lax.axis_size(("z", "x"))
    ring = lax.axis_size("y")
    scale = feature_scale[None, :]
    factor = (0.5 / frame_total) * scale
    with jax.named_scope("project"):
        own, *pieces = project(
            lax.axis_index("x"), lax.axis_size("x"), frames_now, frames_lag, test_matrix, scale
        )
        for k in (2, 1, 3):
            own = own + shifted(pieces[k - 1], "x", -k).astype(F32)
        proj = gather(ring_sum(own, "z").astype(BF16), "x")

    with jax.named_scope("sketch"):
        y = lax.axis_index("y")
        c = lax.axis_index("c")
        terms = (frames_now, frames_lag, factor)
        send, own = cross(c, y, ring, (2,), (2,), proj, *terms)
        send, proj = lax.optimization_barrier((send, proj))
        came = swapped(send, "c", 1)
        (send,) = cross(c, y, ring, (1, 3, 0), (), proj, *terms)
        (piece,) = combine(own, came, 1)
        others = [shifted(piece, "y", -2)]
        came = swapped(send, "c", 1)
        proj, piece = lax.optimization_barrier((proj, piece))
        (own,) = cross(c, y, ring, (), (1, 3, 0), proj, *terms)
        pieces = combine(own, came, 2)
        others += [shifted(pieces[0], "y", -1), shifted(pieces[1], "y", -3)]

    with jax.named_scope("gram"):
        keep, send, mine = gram_of(c[None], own, came, others)
        slab = scatter_sum(keep + swapped(send, "c", 1), "y")
        slab, mine = lax.optimization_barrier((slab, mine))
        whole = gather(mine, "y")
        slab = exact_sum(slab, "x")
        slab = (slab + swapped(slab, "z", 1)) + (swapped(slab, "z", 6) + swapped(slab, "z", 7))
        slab, whole = lax.optimization_barrier((slab, whole))
        slab = slab + swapped(slab, "z", 2)
        gram = gather(gather(slab, "y"), "c")
        gram, whole = lax.optimization_barrier((gram, whole))
        whole = gather(whole, "c")
        upper, high, low = factorize(gram, feature_total**0.5)
    return (basis_of(whole, high, low), upper)


def solution(mesh):
    split = Mesh(mesh.devices.reshape(4, 2, 8, 4), ("y", "c", "z", "x"))
    traj, feat = ("y", "c"), ("z", "x")
    in_specs = (P(traj, feat), P(traj, feat), P(feat, None), P(feat))
    out_specs = (P(feat, None), P())
    return jax.shard_map(
        on_device, mesh=split, in_specs=in_specs, out_specs=out_specs, check_vma=False
    )
```

```python
import jax
import jax.numpy as jnp
from jax import lax
from jax.experimental import pallas as pl
from jax.experimental.pallas import tpu as pltpu
from jax.sharding import Mesh
from jax.sharding import PartitionSpec as P

F32 = jnp.float32
BF16 = jnp.bfloat16
EXACT = lax.Precision.HIGHEST


def shifted(x, axis, by):
    n = lax.axis_size(axis)
    return lax.ppermute(x, axis, [((i + by) % n, i) for i in range(n)])


def swapped(x, axis, mask):
    n = lax.axis_size(axis)
    return lax.ppermute(x, axis, [(i ^ mask, i) for i in range(n)])


def piece(x, index, size):
    return lax.dynamic_slice_in_dim(x, index * size, size, axis=0)


def scatter_sum(x, axis):
    n = lax.axis_size(axis)
    me = lax.axis_index(axis)
    size = x.shape[0] // n
    total = piece(x, me, size).astype(F32)
    for by in (2, 1, 3) if n == 4 else (1,):
        total = total + shifted(piece(x, (me + by) % n, size), axis, n - by).astype(F32)
    return total


def gather(x, axis):
    n = lax.axis_size(axis)
    me = lax.axis_index(axis)
    size = x.shape[0]
    out = jnp.zeros((n * size, x.shape[1]), x.dtype)
    out = lax.dynamic_update_slice_in_dim(out, x, me * size, axis=0)
    for by in (2, 1, 3) if n == 4 else (1,):
        out = lax.dynamic_update_slice_in_dim(out, shifted(x, axis, by), ((me + by) % n) * size, axis=0)
    return out


def ring_sum(x, axis):
    own = x.astype(BF16)
    before = shifted(own, axis, -1).astype(F32)
    after = shifted(own, axis, 1).astype(F32)
    two = x + before
    three = two + after
    far = shifted(three.astype(BF16), axis, 3).astype(F32)
    near = shifted(two.astype(BF16), axis, -2).astype(F32)
    return three + (far + near)


def exact_sum(x, axis):
    return (x + swapped(x, axis, 1)) + (swapped(x, axis, 2) + swapped(x, axis, 3))


def factor_block(tile, lead, size):
    groups = size // 8
    rows = [tile[8 * g : 8 * g + 8, :] for g in range(groups)]
    sub = lax.broadcasted_iota(jnp.int32, (8, 128), 0)
    for q in range(groups):
        first = lead + 8 * q
        column = [
            [jnp.broadcast_to(rows[g][:, first + k : first + k + 1], (8, 128)) for g in range(q, groups)]
            for k in range(8)
        ]
        pivots = jnp.zeros((8, 128), F32)
        for j in range(8):
            pivot = jnp.broadcast_to(column[j][0][j : j + 1, :], (8, 128))
            inverse = 1.0 / pivot
            pivots = jnp.where(sub == j, pivot, pivots)
            factor = [c * inverse for c in column[j]]
            factor[0] = jnp.where(sub > j, factor[0], 0.0)
            for k in range(j + 1, 8):
                top = jnp.broadcast_to(column[k][0][j : j + 1, :], (8, 128))
                column[k] = [c - f * top for c, f in zip(column[k], factor)]
            top = jnp.broadcast_to(rows[q][j : j + 1, :], (8, 128))
            for g in range(q, groups):
                rows[g] = rows[g] - factor[g - q] * top
        rows[q] = rows[q] * lax.rsqrt(pivots)
    return jnp.concatenate(rows, axis=0)


def factor_kernel(scale, gram_ref, upper_ref, high_ref, low_ref, work):
    n = gram_ref.shape[0]
    size = 64
    row = lax.broadcasted_iota(jnp.int32, (n, n), 0)
    col = lax.broadcasted_iota(jnp.int32, (n, n), 1)
    work[:, :n] = gram_ref[...]
    work[:, n:] = jnp.where(row == col, 1.0, 0.0).astype(F32)
    block_row = lax.broadcasted_iota(jnp.int32, (size, 128), 0)
    block_col = lax.broadcasted_iota(jnp.int32, (size, 128), 1)
    for r0 in range(0, n, size):
        r1 = r0 + size
        lead = r0 % 128
        other = (lead + size) % 128
        tile = work[r0:r1, r0 - lead : r0 - lead + 128]
        mine = (block_col >= lead) & (block_col < lead + size)
        tile = jnp.where(mine, tile, jnp.where(block_col - other == block_row, 1.0, 0.0))
        tile = factor_block(tile, lead, size)
        inverse = tile[:, other : other + size]
        panel = jnp.dot(inverse, work[r0:r1, :], precision=EXACT, preferred_element_type=F32)
        work[r0:r1, :] = panel
        if r1 < n:
            work[r1:, :] = work[r1:, :] - lax.dot_general(
                panel[:, r1:n], panel, (((0,), (0,)), ((), ())), precision=EXACT, preferred_element_type=F32
            )
    upper_ref[...] = jnp.where(row <= col, work[:, :n], 0.0)
    inverse = jnp.where(row >= col, work[:, n:], 0.0) * scale
    high = inverse.astype(BF16)
    high_ref[...] = high
    low_ref[...] = (inverse - high.astype(F32)).astype(BF16)


def factorize(gram, scale):
    n = gram.shape[0]
    whole = pl.BlockSpec(memory_space=pltpu.VMEM)
    return pl.pallas_call(
        lambda *refs: factor_kernel(scale, *refs),
        out_shape=[
            jax.ShapeDtypeStruct((n, n), F32),
            jax.ShapeDtypeStruct((n, n), BF16),
            jax.ShapeDtypeStruct((n, n), BF16),
        ],
        in_specs=[whole],
        out_specs=[whole] * 3,
        scratch_shapes=[pltpu.VMEM((n, 2 * n), F32)],
        compiler_params=pltpu.CompilerParams(vmem_limit_bytes=16 * 2**20),
        cost_estimate=pl.CostEstimate(flops=12 * n * n * n, bytes_accessed=8 * n * n, transcendentals=0),
        name="factorize",
    )(gram)


def in_hbm(x):
    return pltpu.with_memory_space_constraint(x, pltpu.HBM)


def project_kernel(parts, me_ref, now_hbm, lag_hbm, test_hbm, scale_hbm, *refs):
    *piece_refs, frames_both, test, scale_ref, total, sems = refs
    frames, features = now_hbm.shape
    columns = test.shape[1]
    width = features // parts
    copies = []
    scales = pltpu.make_async_copy(scale_hbm, scale_ref, sems.at[3 * parts])
    scales.start()
    for i in range(parts):
        at = pl.ds(i * width, width)
        copies.append(
            [
                pltpu.make_async_copy(test_hbm.at[at], test.at[at], sems.at[3 * i]),
                pltpu.make_async_copy(now_hbm.at[:, at], frames_both.at[pl.ds(0, frames), at], sems.at[3 * i + 1]),
                pltpu.make_async_copy(lag_hbm.at[:, at], frames_both.at[pl.ds(frames, frames), at], sems.at[3 * i + 2]),
            ]
        )
        for copy in copies[-1]:
            copy.start()
    scales.wait()
    for i in range(parts):
        copies[i][0].wait()
        scaled = [
            (jnp.transpose(test[r : r + 128, :]).astype(F32) * scale_ref[:, r : r + 128]).astype(BF16)
            for r in range(i * width, (i + 1) * width, 128)
        ]
        scaled = jnp.concatenate(scaled, axis=1)
        copies[i][1].wait()
        copies[i][2].wait()
        term = lax.dot_general(
            scaled,
            frames_both[:, i * width : (i + 1) * width],
            (((1,), (1,)), ((), ())),
            preferred_element_type=F32,
        )
        total[...] = term if i == 0 else total[...] + term
    count = len(piece_refs)
    size = columns // count
    for k, piece_ref in enumerate(piece_refs):
        at = pl.multiple_of(lax.rem(me_ref[0] + k, count) * size, size)
        piece_ref[...] = total[pl.ds(at, size), :].astype(piece_ref.dtype)


def project(me, count, frames_now, frames_lag, test_matrix, scale):
    frames, features = frames_now.shape
    columns = test_matrix.shape[1]
    parts = 4
    size = columns // count
    vmem = pl.BlockSpec(memory_space=pltpu.VMEM)
    hbm = pl.BlockSpec(memory_space=pl.ANY)
    return pl.pallas_call(
        lambda *refs: project_kernel(parts, *refs),
        in_specs=[pl.BlockSpec(memory_space=pltpu.SMEM), hbm, hbm, hbm, hbm],
        out_specs=[vmem] * count,
        out_shape=[jax.ShapeDtypeStruct((size, 2 * frames), F32)]
        + [jax.ShapeDtypeStruct((size, 2 * frames), BF16)] * (count - 1),
        scratch_shapes=[
            pltpu.VMEM((2 * frames, features), BF16),
            pltpu.VMEM((features, columns), BF16),
            pltpu.VMEM((1, features), F32),
            pltpu.VMEM((columns, 2 * frames), F32),
            pltpu.SemaphoreType.DMA((3 * parts + 1,)),
        ],
        compiler_params=pltpu.CompilerParams(vmem_limit_bytes=32 * 2**20),
        cost_estimate=pl.CostEstimate(
            flops=4 * frames * features * columns, bytes_accessed=4 * frames * features, transcendentals=0
        ),
        name="project",
    )(me[None], in_hbm(frames_now), in_hbm(frames_lag), in_hbm(test_matrix), in_hbm(scale))


def cross_kernel(jobs, where_ref, proj_ref, now_hbm, lag_hbm, factor_ref, *refs):
    *out_refs, work, sems = refs
    frames = now_hbm.shape[0]
    block = out_refs[0].shape[2]
    count = now_hbm.shape[1] // (2 * block)
    places = []
    copies = []
    for n, (_, _, other, slot) in enumerate(jobs):
        half = 1 - where_ref[0] if other else where_ref[0]
        first = half * count + lax.rem(where_ref[1] + slot, count)
        at = pl.ds(pl.multiple_of(first * block, block), block)
        places.append(at)
        copies.append(
            [
                pltpu.make_async_copy(now_hbm.at[:, at], work.at[n, pl.ds(0, frames)], sems.at[2 * n]),
                pltpu.make_async_copy(lag_hbm.at[:, at], work.at[n, pl.ds(frames, frames)], sems.at[2 * n + 1]),
            ]
        )
        for copy in copies[-1]:
            copy.start()
    proj = jnp.concatenate([proj_ref[:, frames:], proj_ref[:, :frames]], axis=1)
    for n, (out, row, _, _) in enumerate(jobs):
        for copy in copies[n]:
            copy.wait()
        total = jnp.dot(proj, work[n], preferred_element_type=F32)
        out_refs[out][row] = (total * factor_ref[:, places[n]]).astype(out_refs[out].dtype)


def cross(core, ring_place, ring, slots_other, slots_own, proj, frames_now, frames_lag, factor):
    frames, features = frames_now.shape
    columns = proj.shape[0]
    block = features // (2 * ring)
    jobs, out_shape = [], []
    for slots, other, dtype in ((slots_other, True, BF16), (slots_own, False, F32)):
        if slots:
            jobs += [(len(out_shape), row, other, slot) for row, slot in enumerate(slots)]
            out_shape.append(jax.ShapeDtypeStruct((len(slots), columns, block), dtype))
    vmem = pl.BlockSpec(memory_space=pltpu.VMEM)
    hbm = pl.BlockSpec(memory_space=pl.ANY)
    return pl.pallas_call(
        lambda *refs: cross_kernel(jobs, *refs),
        in_specs=[pl.BlockSpec(memory_space=pltpu.SMEM), vmem, hbm, hbm, vmem],
        out_specs=[vmem] * len(out_shape),
        out_shape=out_shape,
        scratch_shapes=[
            pltpu.VMEM((len(jobs), 2 * frames, block), BF16),
            pltpu.SemaphoreType.DMA((2 * len(jobs),)),
        ],
        compiler_params=pltpu.CompilerParams(vmem_limit_bytes=24 * 2**20),
        cost_estimate=pl.CostEstimate(
            flops=4 * frames * len(jobs) * block * columns,
            bytes_accessed=4 * frames * len(jobs) * block,
            transcendentals=0,
        ),
        name="cross",
    )(jnp.stack([core, ring_place]), proj, in_hbm(frames_now), in_hbm(frames_lag), factor)


def combine_kernel(own_ref, came_ref, *out_refs):
    for k, out_ref in enumerate(out_refs):
        out_ref[...] = (own_ref[k] + came_ref[k].astype(F32)).astype(BF16)


def combine(own, came, count):
    _, columns, block = own.shape
    whole = pl.BlockSpec(memory_space=pltpu.VMEM)
    return pl.pallas_call(
        combine_kernel,
        in_specs=[whole] * 2,
        out_specs=[whole] * count,
        out_shape=[jax.ShapeDtypeStruct((columns, block), BF16)] * count,
        compiler_params=pltpu.CompilerParams(vmem_limit_bytes=16 * 2**20),
        name="combine",
    )(own, came)


def gram_kernel(core_ref, own_ref, came_ref, a_ref, b_ref, d_ref, keep_ref, send_ref, rows_ref, work):
    total = own_ref[own_ref.shape[0] - 1] + came_ref[own_ref.shape[0] - 1].astype(F32)
    total = total + (a_ref[...].astype(F32) + b_ref[...].astype(F32) + d_ref[...].astype(F32))
    half = keep_ref.shape[0]
    core = core_ref[0]
    work[...] = lax.dot_general(
        total, total, (((1,), (1,)), ((), ())), precision=EXACT, preferred_element_type=F32
    )
    keep_ref[...] = work[pl.ds(pl.multiple_of(core * half, half), half), :]
    send_ref[...] = work[pl.ds(pl.multiple_of((1 - core) * half, half), half), :]
    rows_ref[...] = jnp.transpose(total).astype(BF16)


def gram_of(core, own, came, others):
    columns, block = own.shape[1:]
    whole = pl.BlockSpec(memory_space=pltpu.VMEM)
    half = jax.ShapeDtypeStruct((columns // 2, columns), F32)
    return pl.pallas_call(
        gram_kernel,
        in_specs=[pl.BlockSpec(memory_space=pltpu.SMEM)] + [whole] * 5,
        out_specs=[whole] * 3,
        out_shape=[half, half, jax.ShapeDtypeStruct((block, columns), BF16)],
        scratch_shapes=[pltpu.VMEM((columns, columns), F32)],
        compiler_params=pltpu.CompilerParams(vmem_limit_bytes=16 * 2**20),
        name="gram",
    )(core, own, came, *others)


def basis_kernel(parts, sketch_ref, high_ref, low_ref, out_hbm, work, sems):
    transposed = (((1,), (1,)), ((), ()))
    size = work.shape[0] // parts
    copies = []
    for i in range(parts):
        at = slice(i * size, (i + 1) * size)
        total = lax.dot_general(sketch_ref[at, :], high_ref[...], transposed, preferred_element_type=F32)
        total = total + lax.dot_general(sketch_ref[at, :], low_ref[...], transposed, preferred_element_type=F32)
        work[at, :] = total.astype(BF16)
        rows = pl.ds(i * size, size)
        copies.append(pltpu.make_async_copy(work.at[rows], out_hbm.at[rows], sems.at[i]))
        copies[-1].start()
    for copy in copies:
        copy.wait()


def basis_of(sketch, high, low):
    rows, columns = sketch.shape
    parts = 8
    vmem = pl.BlockSpec(memory_space=pltpu.VMEM)
    return pl.pallas_call(
        lambda *refs: basis_kernel(parts, *refs),
        in_specs=[vmem] * 3,
        out_specs=pl.BlockSpec(memory_space=pl.ANY),
        out_shape=jax.ShapeDtypeStruct((rows, columns), BF16),
        scratch_shapes=[pltpu.VMEM((rows, columns), BF16), pltpu.SemaphoreType.DMA((parts,))],
        compiler_params=pltpu.CompilerParams(vmem_limit_bytes=16 * 2**20),
        cost_estimate=pl.CostEstimate(
            flops=4 * rows * columns * columns, bytes_accessed=4 * rows * columns, transcendentals=0
        ),
        name="basis",
    )(sketch, high, low)


def on_device(frames_now, frames_lag, test_matrix, feature_scale):
    frames, features = frames_now.shape
    frame_total = frames * lax.axis_size(("y", "c"))
    feature_total = features * lax.axis_size(("z", "x"))
    ring = lax.axis_size("y")
    scale = feature_scale[None, :]
    factor = (0.5 / frame_total) * scale
    with jax.named_scope("project"):
        own, *pieces = project(
            lax.axis_index("x"), lax.axis_size("x"), frames_now, frames_lag, test_matrix, scale
        )
        for k in (2, 1, 3):
            own = own + shifted(pieces[k - 1], "x", -k).astype(F32)
        proj = gather(ring_sum(own, "z").astype(BF16), "x")

    with jax.named_scope("sketch"):
        y = lax.axis_index("y")
        c = lax.axis_index("c")
        terms = (frames_now, frames_lag, factor)
        send, own = cross(c, y, ring, (2,), (2,), proj, *terms)
        send, proj = lax.optimization_barrier((send, proj))
        came = swapped(send, "c", 1)
        (send,) = cross(c, y, ring, (1, 3, 0), (), proj, *terms)
        (piece,) = combine(own, came, 1)
        send, proj, piece = lax.optimization_barrier((send, proj, piece))
        others = [shifted(piece, "y", -2)]
        came = swapped(send, "c", 1)
        (own,) = cross(c, y, ring, (), (1, 3, 0), proj, *terms)
        pieces = combine(own, came, 2)
        others += [shifted(pieces[0], "y", -1), shifted(pieces[1], "y", -3)]

    with jax.named_scope("gram"):
        keep, send, mine = gram_of(c[None], own, came, others)
        slab = scatter_sum(keep + swapped(send, "c", 1), "y")
        slab, mine = lax.optimization_barrier((slab, mine))
        whole = gather(mine, "y")
        slab = exact_sum(slab, "x")
        slab = (slab + swapped(slab, "z", 1)) + (swapped(slab, "z", 6) + swapped(slab, "z", 7))
        slab, whole = lax.optimization_barrier((slab, whole))
        slab = slab + swapped(slab, "z", 2)
        gram = gather(gather(slab, "y"), "c")
        gram, whole = lax.optimization_barrier((gram, whole))
        whole = gather(whole, "c")
        upper, high, low = factorize(gram, feature_total**0.5)
    return (basis_of(whole, high, low), upper)


def solution(mesh):
    split = Mesh(mesh.devices.reshape(4, 2, 8, 4), ("y", "c", "z", "x"))
    traj, feat = ("y", "c"), ("z", "x")
    in_specs = (P(traj, feat), P(traj, feat), P(feat, None), P(feat))
    out_specs = (P(feat, None), P())
    return jax.shard_map(
        on_device, mesh=split, in_specs=in_specs, out_specs=out_specs, check_vma=False
    )
```

```python
import jax
import jax.numpy as jnp
from jax import lax
from jax.experimental import pallas as pl
from jax.experimental.pallas import tpu as pltpu
from jax.sharding import Mesh
from jax.sharding import PartitionSpec as P

F32 = jnp.float32
BF16 = jnp.bfloat16
EXACT = lax.Precision.HIGHEST


def shifted(x, axis, by):
    n = lax.axis_size(axis)
    return lax.ppermute(x, axis, [((i + by) % n, i) for i in range(n)])


def swapped(x, axis, mask):
    n = lax.axis_size(axis)
    return lax.ppermute(x, axis, [(i ^ mask, i) for i in range(n)])


def piece(x, index, size):
    return lax.dynamic_slice_in_dim(x, index * size, size, axis=0)


def scatter_sum(x, axis):
    n = lax.axis_size(axis)
    me = lax.axis_index(axis)
    size = x.shape[0] // n
    total = piece(x, me, size).astype(F32)
    for by in (2, 1, 3) if n == 4 else (1,):
        total = total + shifted(piece(x, (me + by) % n, size), axis, n - by).astype(F32)
    return total


def placed(pieces, axis):
    n = len(pieces)
    me = lax.axis_index(axis)
    size = pieces[0].shape[0]
    out = jnp.zeros((n * size, pieces[0].shape[1]), pieces[0].dtype)
    for k, piece_k in enumerate(pieces):
        out = lax.dynamic_update_slice_in_dim(out, piece_k, ((me + k) % n) * size, axis=0)
    return out


def gather(x, axis):
    n = lax.axis_size(axis)
    came = {k: shifted(x, axis, k) for k in ((2, 1, 3) if n == 4 else (1,))}
    return placed([x] + [came[k] for k in range(1, n)], axis)


def ring_sum(x, axis):
    own = x.astype(BF16)
    before = shifted(own, axis, -1).astype(F32)
    after = shifted(own, axis, 1).astype(F32)
    two = x + before
    three = two + after
    far = shifted(three.astype(BF16), axis, 3).astype(F32)
    near = shifted(two.astype(BF16), axis, -2).astype(F32)
    return three + (far + near)


def exact_sum(x, axis, masks):
    came = [swapped(x, axis, mask) for mask in masks]
    return x + came[0] if len(came) == 1 else (x + came[0]) + (came[1] + came[2])


def factor_block(tile, lead, size):
    groups = size // 8
    rows = [tile[8 * g : 8 * g + 8, :] for g in range(groups)]
    sub = lax.broadcasted_iota(jnp.int32, (8, 128), 0)
    for q in range(groups):
        first = lead + 8 * q
        column = [
            [jnp.broadcast_to(rows[g][:, first + k : first + k + 1], (8, 128)) for g in range(q, groups)]
            for k in range(8)
        ]
        pivots = jnp.zeros((8, 128), F32)
        for j in range(8):
            pivot = jnp.broadcast_to(column[j][0][j : j + 1, :], (8, 128))
            inverse = 1.0 / pivot
            pivots = jnp.where(sub == j, pivot, pivots)
            factor = [c * inverse for c in column[j]]
            factor[0] = jnp.where(sub > j, factor[0], 0.0)
            for k in range(j + 1, 8):
                top = jnp.broadcast_to(column[k][0][j : j + 1, :], (8, 128))
                column[k] = [c - f * top for c, f in zip(column[k], factor)]
            top = jnp.broadcast_to(rows[q][j : j + 1, :], (8, 128))
            for g in range(q, groups):
                rows[g] = rows[g] - factor[g - q] * top
        rows[q] = rows[q] * lax.rsqrt(pivots)
    return jnp.concatenate(rows, axis=0)


def factor_kernel(scale, gram_ref, upper_ref, high_ref, low_ref, work):
    n = gram_ref.shape[0]
    size = 64
    row = lax.broadcasted_iota(jnp.int32, (n, n), 0)
    col = lax.broadcasted_iota(jnp.int32, (n, n), 1)
    work[:, :n] = gram_ref[...]
    work[:, n:] = jnp.where(row == col, 1.0, 0.0).astype(F32)
    block_row = lax.broadcasted_iota(jnp.int32, (size, 128), 0)
    block_col = lax.broadcasted_iota(jnp.int32, (size, 128), 1)
    for r0 in range(0, n, size):
        r1 = r0 + size
        lead = r0 % 128
        other = (lead + size) % 128
        tile = work[r0:r1, r0 - lead : r0 - lead + 128]
        mine = (block_col >= lead) & (block_col < lead + size)
        tile = jnp.where(mine, tile, jnp.where(block_col - other == block_row, 1.0, 0.0))
        tile = factor_block(tile, lead, size)
        inverse = tile[:, other : other + size]
        panel = jnp.dot(inverse, work[r0:r1, :], precision=EXACT, preferred_element_type=F32)
        work[r0:r1, :] = panel
        if r1 < n:
            work[r1:, :] = work[r1:, :] - lax.dot_general(
                panel[:, r1:n], panel, (((0,), (0,)), ((), ())), precision=EXACT, preferred_element_type=F32
            )
    upper_ref[...] = jnp.where(row <= col, work[:, :n], 0.0)
    inverse = jnp.where(row >= col, work[:, n:], 0.0) * scale
    high = inverse.astype(BF16)
    high_ref[...] = high
    low_ref[...] = (inverse - high.astype(F32)).astype(BF16)


def factorize(gram, scale):
    n = gram.shape[0]
    whole = pl.BlockSpec(memory_space=pltpu.VMEM)
    return pl.pallas_call(
        lambda *refs: factor_kernel(scale, *refs),
        out_shape=[
            jax.ShapeDtypeStruct((n, n), F32),
            jax.ShapeDtypeStruct((n, n), BF16),
            jax.ShapeDtypeStruct((n, n), BF16),
        ],
        in_specs=[whole],
        out_specs=[whole] * 3,
        scratch_shapes=[pltpu.VMEM((n, 2 * n), F32)],
        compiler_params=pltpu.CompilerParams(vmem_limit_bytes=16 * 2**20),
        cost_estimate=pl.CostEstimate(flops=12 * n * n * n, bytes_accessed=8 * n * n, transcendentals=0),
        name="factorize",
    )(gram)


def in_hbm(x):
    return pltpu.with_memory_space_constraint(x, pltpu.HBM)


def project_kernel(parts, me_ref, now_hbm, lag_hbm, test_hbm, scale_hbm, *refs):
    *piece_refs, frames_both, test, scale_ref, total, sems = refs
    frames, features = now_hbm.shape
    columns = test.shape[1]
    width = features // parts
    copies = []
    scales = pltpu.make_async_copy(scale_hbm, scale_ref, sems.at[3 * parts])
    scales.start()
    for i in range(parts):
        at = pl.ds(i * width, width)
        copies.append(
            [
                pltpu.make_async_copy(test_hbm.at[at], test.at[at], sems.at[3 * i]),
                pltpu.make_async_copy(now_hbm.at[:, at], frames_both.at[pl.ds(0, frames), at], sems.at[3 * i + 1]),
                pltpu.make_async_copy(lag_hbm.at[:, at], frames_both.at[pl.ds(frames, frames), at], sems.at[3 * i + 2]),
            ]
        )
        for copy in copies[-1]:
            copy.start()
    scales.wait()
    for i in range(parts):
        copies[i][0].wait()
        scaled = [
            (jnp.transpose(test[r : r + 128, :]).astype(F32) * scale_ref[:, r : r + 128]).astype(BF16)
            for r in range(i * width, (i + 1) * width, 128)
        ]
        scaled = jnp.concatenate(scaled, axis=1)
        copies[i][1].wait()
        copies[i][2].wait()
        term = lax.dot_general(
            scaled,
            frames_both[:, i * width : (i + 1) * width],
            (((1,), (1,)), ((), ())),
            preferred_element_type=F32,
        )
        total[...] = term if i == 0 else total[...] + term
    count = len(piece_refs)
    size = columns // count
    for k, piece_ref in enumerate(piece_refs):
        at = pl.multiple_of(lax.rem(me_ref[0] + k, count) * size, size)
        piece_ref[...] = total[pl.ds(at, size), :].astype(piece_ref.dtype)


def project(me, count, frames_now, frames_lag, test_matrix, scale):
    frames, features = frames_now.shape
    columns = test_matrix.shape[1]
    parts = 4
    size = columns // count
    vmem = pl.BlockSpec(memory_space=pltpu.VMEM)
    hbm = pl.BlockSpec(memory_space=pl.ANY)
    return pl.pallas_call(
        lambda *refs: project_kernel(parts, *refs),
        in_specs=[pl.BlockSpec(memory_space=pltpu.SMEM), hbm, hbm, hbm, hbm],
        out_specs=[vmem] * count,
        out_shape=[jax.ShapeDtypeStruct((size, 2 * frames), F32)]
        + [jax.ShapeDtypeStruct((size, 2 * frames), BF16)] * (count - 1),
        scratch_shapes=[
            pltpu.VMEM((2 * frames, features), BF16),
            pltpu.VMEM((features, columns), BF16),
            pltpu.VMEM((1, features), F32),
            pltpu.VMEM((columns, 2 * frames), F32),
            pltpu.SemaphoreType.DMA((3 * parts + 1,)),
        ],
        compiler_params=pltpu.CompilerParams(vmem_limit_bytes=32 * 2**20),
        cost_estimate=pl.CostEstimate(
            flops=4 * frames * features * columns, bytes_accessed=4 * frames * features, transcendentals=0
        ),
        name="project",
    )(me[None], in_hbm(frames_now), in_hbm(frames_lag), in_hbm(test_matrix), in_hbm(scale))


def cross_kernel(jobs, where_ref, proj_ref, now_hbm, lag_hbm, factor_ref, *refs):
    *out_refs, work, sems = refs
    frames = now_hbm.shape[0]
    block = out_refs[0].shape[2]
    count = now_hbm.shape[1] // (2 * block)
    places = []
    copies = []
    for n, (_, _, other, slot) in enumerate(jobs):
        half = 1 - where_ref[0] if other else where_ref[0]
        first = half * count + lax.rem(where_ref[1] + slot, count)
        at = pl.ds(pl.multiple_of(first * block, block), block)
        places.append(at)
        copies.append(
            [
                pltpu.make_async_copy(now_hbm.at[:, at], work.at[n, pl.ds(0, frames)], sems.at[2 * n]),
                pltpu.make_async_copy(lag_hbm.at[:, at], work.at[n, pl.ds(frames, frames)], sems.at[2 * n + 1]),
            ]
        )
        for copy in copies[-1]:
            copy.start()
    proj = jnp.concatenate([proj_ref[:, frames:], proj_ref[:, :frames]], axis=1)
    for n, (out, row, _, _) in enumerate(jobs):
        for copy in copies[n]:
            copy.wait()
        total = jnp.dot(proj, work[n], preferred_element_type=F32)
        out_refs[out][row] = (total * factor_ref[:, places[n]]).astype(out_refs[out].dtype)


def cross(core, ring_place, ring, slots_other, slots_own, proj, frames_now, frames_lag, factor):
    frames, features = frames_now.shape
    columns = proj.shape[0]
    block = features // (2 * ring)
    jobs, out_shape = [], []
    for slots, other, dtype in ((slots_other, True, BF16), (slots_own, False, F32)):
        if slots:
            jobs += [(len(out_shape), row, other, slot) for row, slot in enumerate(slots)]
            out_shape.append(jax.ShapeDtypeStruct((len(slots), columns, block), dtype))
    vmem = pl.BlockSpec(memory_space=pltpu.VMEM)
    hbm = pl.BlockSpec(memory_space=pl.ANY)
    return pl.pallas_call(
        lambda *refs: cross_kernel(jobs, *refs),
        in_specs=[pl.BlockSpec(memory_space=pltpu.SMEM), vmem, hbm, hbm, vmem],
        out_specs=[vmem] * len(out_shape),
        out_shape=out_shape,
        scratch_shapes=[
            pltpu.VMEM((len(jobs), 2 * frames, block), BF16),
            pltpu.SemaphoreType.DMA((2 * len(jobs),)),
        ],
        compiler_params=pltpu.CompilerParams(vmem_limit_bytes=24 * 2**20),
        cost_estimate=pl.CostEstimate(
            flops=4 * frames * len(jobs) * block * columns,
            bytes_accessed=4 * frames * len(jobs) * block,
            transcendentals=0,
        ),
        name="cross",
    )(jnp.stack([core, ring_place]), proj, in_hbm(frames_now), in_hbm(frames_lag), factor)


def combine_kernel(own_ref, came_ref, *out_refs):
    for k, out_ref in enumerate(out_refs):
        out_ref[...] = (own_ref[k] + came_ref[k].astype(F32)).astype(BF16)


def combine(own, came, count):
    _, columns, block = own.shape
    whole = pl.BlockSpec(memory_space=pltpu.VMEM)
    return pl.pallas_call(
        combine_kernel,
        in_specs=[whole] * 2,
        out_specs=[whole] * count,
        out_shape=[jax.ShapeDtypeStruct((columns, block), BF16)] * count,
        compiler_params=pltpu.CompilerParams(vmem_limit_bytes=16 * 2**20),
        name="combine",
    )(own, came)


def gram_kernel(core_ref, own_ref, came_ref, a_ref, b_ref, d_ref, keep_ref, send_ref, rows_ref, work):
    total = own_ref[own_ref.shape[0] - 1] + came_ref[own_ref.shape[0] - 1].astype(F32)
    total = total + (a_ref[...].astype(F32) + b_ref[...].astype(F32) + d_ref[...].astype(F32))
    half = keep_ref.shape[0]
    core = core_ref[0]
    work[...] = lax.dot_general(
        total, total, (((1,), (1,)), ((), ())), precision=EXACT, preferred_element_type=F32
    )
    keep_ref[...] = work[pl.ds(pl.multiple_of(core * half, half), half), :]
    send_ref[...] = work[pl.ds(pl.multiple_of((1 - core) * half, half), half), :]
    rows_ref[...] = jnp.transpose(total).astype(BF16)


def gram_of(core, own, came, others):
    columns, block = own.shape[1:]
    whole = pl.BlockSpec(memory_space=pltpu.VMEM)
    half = jax.ShapeDtypeStruct((columns // 2, columns), F32)
    return pl.pallas_call(
        gram_kernel,
        in_specs=[pl.BlockSpec(memory_space=pltpu.SMEM)] + [whole] * 5,
        out_specs=[whole] * 3,
        out_shape=[half, half, jax.ShapeDtypeStruct((block, columns), BF16)],
        scratch_shapes=[pltpu.VMEM((columns, columns), F32)],
        compiler_params=pltpu.CompilerParams(vmem_limit_bytes=16 * 2**20),
        name="gram",
    )(core, own, came, *others)


def basis_kernel(parts, sketch_ref, high_ref, low_ref, out_hbm, work, sems):
    transposed = (((1,), (1,)), ((), ()))
    size = work.shape[0] // parts
    copies = []
    for i in range(parts):
        at = slice(i * size, (i + 1) * size)
        total = lax.dot_general(sketch_ref[at, :], high_ref[...], transposed, preferred_element_type=F32)
        total = total + lax.dot_general(sketch_ref[at, :], low_ref[...], transposed, preferred_element_type=F32)
        work[at, :] = total.astype(BF16)
        rows = pl.ds(i * size, size)
        copies.append(pltpu.make_async_copy(work.at[rows], out_hbm.at[rows], sems.at[i]))
        copies[-1].start()
    for copy in copies:
        copy.wait()


def basis_of(sketch, high, low):
    rows, columns = sketch.shape
    parts = 8
    vmem = pl.BlockSpec(memory_space=pltpu.VMEM)
    return pl.pallas_call(
        lambda *refs: basis_kernel(parts, *refs),
        in_specs=[vmem] * 3,
        out_specs=pl.BlockSpec(memory_space=pl.ANY),
        out_shape=jax.ShapeDtypeStruct((rows, columns), BF16),
        scratch_shapes=[pltpu.VMEM((rows, columns), BF16), pltpu.SemaphoreType.DMA((parts,))],
        compiler_params=pltpu.CompilerParams(vmem_limit_bytes=16 * 2**20),
        cost_estimate=pl.CostEstimate(
            flops=4 * rows * columns * columns, bytes_accessed=4 * rows * columns, transcendentals=0
        ),
        name="basis",
    )(sketch, high, low)


def on_device(frames_now, frames_lag, test_matrix, feature_scale):
    frames, features = frames_now.shape
    frame_total = frames * lax.axis_size(("y", "c"))
    feature_total = features * lax.axis_size(("z", "x"))
    ring = lax.axis_size("y")
    scale = feature_scale[None, :]
    factor = (0.5 / frame_total) * scale
    with jax.named_scope("project"):
        own, *pieces = project(
            lax.axis_index("x"), lax.axis_size("x"), frames_now, frames_lag, test_matrix, scale
        )
        for k in (2, 1, 3):
            own = own + shifted(pieces[k - 1], "x", -k).astype(F32)
        proj = gather(ring_sum(own, "z").astype(BF16), "x")

    with jax.named_scope("sketch"):
        y = lax.axis_index("y")
        c = lax.axis_index("c")
        terms = (frames_now, frames_lag, factor)
        send, own = cross(c, y, ring, (2,), (2,), proj, *terms)
        send, proj = lax.optimization_barrier((send, proj))
        came = swapped(send, "c", 1)
        (send,) = cross(c, y, ring, (1, 3, 0), (), proj, *terms)
        (piece,) = combine(own, came, 1)
        send, proj, piece = lax.optimization_barrier((send, proj, piece))
        others = [shifted(piece, "y", -2)]
        came = swapped(send, "c", 1)
        (own,) = cross(c, y, ring, (), (1, 3, 0), proj, *terms)
        pieces = combine(own, came, 2)
        others += [shifted(pieces[0], "y", -1), shifted(pieces[1], "y", -3)]

    with jax.named_scope("gram"):
        keep, send, mine = gram_of(c[None], own, came, others)
        slab = keep + swapped(send, "c", 1)
        slab, mine = lax.optimization_barrier((slab, mine))
        across = shifted(mine, "y", 2)
        slab = scatter_sum(slab, "x")
        slab, across = lax.optimization_barrier((slab, across))
        ahead, behind = shifted(mine, "y", 1), shifted(mine, "y", -1)
        slab = exact_sum(slab, "z", (1, 6, 7))
        slab = exact_sum(slab, "z", (2,))
        slab, ahead, behind = lax.optimization_barrier((slab, ahead, behind))
        slab = exact_sum(slab, "y", (1, 2, 3))
        gram = gather(gather(slab, "x"), "c")
        whole = placed((mine, ahead, across, behind), "y")
        gram, whole = lax.optimization_barrier((gram, whole))
        whole = gather(whole, "c")
        upper, high, low = factorize(gram, feature_total**0.5)
    return (basis_of(whole, high, low), upper)


def solution(mesh):
    split = Mesh(mesh.devices.reshape(4, 2, 8, 4), ("y", "c", "z", "x"))
    traj, feat = ("y", "c"), ("z", "x")
    in_specs = (P(traj, feat), P(traj, feat), P(feat, None), P(feat))
    out_specs = (P(feat, None), P())
    return jax.shard_map(
        on_device, mesh=split, in_specs=in_specs, out_specs=out_specs, check_vma=False
    )
```

```python
import jax
import jax.numpy as jnp
from jax import lax
from jax.experimental import pallas as pl
from jax.experimental.pallas import tpu as pltpu
from jax.sharding import Mesh
from jax.sharding import PartitionSpec as P

F32 = jnp.float32
BF16 = jnp.bfloat16
EXACT = lax.Precision.HIGHEST


def moved(x, axis, source, core):
    n = lax.axis_size(axis)
    if core is None:
        return lax.ppermute(x, axis, [(source(i, n), i) for i in range(n)])
    if axis == "y":
        return lax.ppermute(x, (axis, "c"), [(2 * source(i, n) + core, 2 * i + core) for i in range(n)])
    return lax.ppermute(x, ("c", axis), [(core * n + source(i, n), core * n + i) for i in range(n)])


def shifted(x, axis, by, core=None):
    return moved(x, axis, lambda i, n: (i + by) % n, core)


def swapped(x, axis, mask, core=None):
    return moved(x, axis, lambda i, n: i ^ mask, core)


def piece(x, index, size):
    return lax.dynamic_slice_in_dim(x, index * size, size, axis=0)


def scatter_sum(x, axis, core):
    n = lax.axis_size(axis)
    me = lax.axis_index(axis)
    size = x.shape[0] // n
    total = piece(x, me, size)
    for by in (2, 1, 3):
        total = total + shifted(piece(x, (me + by) % n, size), axis, n - by, core)
    return total


def placed(pieces, axis, dim=0):
    n = len(pieces)
    me = lax.axis_index(axis)
    shape = list(pieces[0].shape)
    size = shape[dim]
    shape[dim] = n * size
    out = jnp.zeros(shape, pieces[0].dtype)
    for k, piece_k in enumerate(pieces):
        out = lax.dynamic_update_slice_in_dim(out, piece_k, ((me + k) % n) * size, axis=dim)
    return out


def gather(x, axis, core=None, dim=0):
    came = {k: shifted(x, axis, k, core) for k in (2, 1, 3)}
    return placed([x] + [came[k] for k in (1, 2, 3)], axis, dim)


def ring_sum(x, axis):
    own = x.astype(BF16)
    before = shifted(own, axis, -1).astype(F32)
    after = shifted(own, axis, 1).astype(F32)
    two = x + before
    three = two + after
    far = shifted(three.astype(BF16), axis, 3).astype(F32)
    near = shifted(two.astype(BF16), axis, -2).astype(F32)
    return three + (far + near)


def exact_sum(x, axis, masks, core):
    came = [swapped(x, axis, mask, core) for mask in masks]
    return x + came[0] if len(came) == 1 else (x + came[0]) + (came[1] + came[2])


def factor_block(tile, lead, size):
    groups = size // 8
    rows = [tile[8 * g : 8 * g + 8, :] for g in range(groups)]
    sub = lax.broadcasted_iota(jnp.int32, (8, 128), 0)
    for q in range(groups):
        first = lead + 8 * q
        column = [
            [jnp.broadcast_to(rows[g][:, first + k : first + k + 1], (8, 128)) for g in range(q, groups)]
            for k in range(8)
        ]
        pivots = jnp.zeros((8, 128), F32)
        for j in range(8):
            pivot = jnp.broadcast_to(column[j][0][j : j + 1, :], (8, 128))
            inverse = 1.0 / pivot
            pivots = jnp.where(sub == j, pivot, pivots)
            factor = [c * inverse for c in column[j]]
            factor[0] = jnp.where(sub > j, factor[0], 0.0)
            for k in range(j + 1, 8):
                top = jnp.broadcast_to(column[k][0][j : j + 1, :], (8, 128))
                column[k] = [c - f * top for c, f in zip(column[k], factor)]
            top = jnp.broadcast_to(rows[q][j : j + 1, :], (8, 128))
            for g in range(q, groups):
                rows[g] = rows[g] - factor[g - q] * top
        rows[q] = rows[q] * lax.rsqrt(pivots)
    return jnp.concatenate(rows, axis=0)


def factor_kernel(scale, gram_ref, upper_ref, high_ref, low_ref, work):
    n = gram_ref.shape[0]
    size = 64
    row = lax.broadcasted_iota(jnp.int32, (n, n), 0)
    col = lax.broadcasted_iota(jnp.int32, (n, n), 1)
    work[:, :n] = gram_ref[...]
    work[:, n:] = jnp.where(row == col, 1.0, 0.0).astype(F32)
    block_row = lax.broadcasted_iota(jnp.int32, (size, 128), 0)
    block_col = lax.broadcasted_iota(jnp.int32, (size, 128), 1)
    for r0 in range(0, n, size):
        r1 = r0 + size
        lead = r0 % 128
        other = (lead + size) % 128
        tile = work[r0:r1, r0 - lead : r0 - lead + 128]
        mine = (block_col >= lead) & (block_col < lead + size)
        tile = jnp.where(mine, tile, jnp.where(block_col - other == block_row, 1.0, 0.0))
        tile = factor_block(tile, lead, size)
        inverse = tile[:, other : other + size]
        panel = jnp.dot(inverse, work[r0:r1, :], precision=EXACT, preferred_element_type=F32)
        work[r0:r1, :] = panel
        if r1 < n:
            work[r1:, :] = work[r1:, :] - lax.dot_general(
                panel[:, r1:n], panel, (((0,), (0,)), ((), ())), precision=EXACT, preferred_element_type=F32
            )
    upper_ref[...] = jnp.where(row <= col, work[:, :n], 0.0)
    inverse = jnp.where(row >= col, work[:, n:], 0.0) * scale
    high = inverse.astype(BF16)
    high_ref[...] = high
    low_ref[...] = (inverse - high.astype(F32)).astype(BF16)


def factorize(gram, scale):
    n = gram.shape[0]
    whole = pl.BlockSpec(memory_space=pltpu.VMEM)
    return pl.pallas_call(
        lambda *refs: factor_kernel(scale, *refs),
        out_shape=[
            jax.ShapeDtypeStruct((n, n), F32),
            jax.ShapeDtypeStruct((n, n), BF16),
            jax.ShapeDtypeStruct((n, n), BF16),
        ],
        in_specs=[whole],
        out_specs=[whole] * 3,
        scratch_shapes=[pltpu.VMEM((n, 2 * n), F32)],
        compiler_params=pltpu.CompilerParams(vmem_limit_bytes=16 * 2**20),
        cost_estimate=pl.CostEstimate(flops=12 * n * n * n, bytes_accessed=8 * n * n, transcendentals=0),
        name="factorize",
    )(gram)


def in_hbm(x):
    return pltpu.with_memory_space_constraint(x, pltpu.HBM)


def project_kernel(parts, me_ref, now_hbm, lag_hbm, test_hbm, scale_hbm, *refs):
    *piece_refs, frames_both, test, scale_ref, total, sems = refs
    frames, features = now_hbm.shape
    columns = test.shape[1]
    width = features // parts
    copies = []
    scales = pltpu.make_async_copy(scale_hbm, scale_ref, sems.at[3 * parts])
    scales.start()
    for i in range(parts):
        at = pl.ds(i * width, width)
        copies.append(
            [
                pltpu.make_async_copy(test_hbm.at[at], test.at[at], sems.at[3 * i]),
                pltpu.make_async_copy(now_hbm.at[:, at], frames_both.at[pl.ds(0, frames), at], sems.at[3 * i + 1]),
                pltpu.make_async_copy(lag_hbm.at[:, at], frames_both.at[pl.ds(frames, frames), at], sems.at[3 * i + 2]),
            ]
        )
        for copy in copies[-1]:
            copy.start()
    scales.wait()
    for i in range(parts):
        copies[i][0].wait()
        scaled = [
            (jnp.transpose(test[r : r + 128, :]).astype(F32) * scale_ref[:, r : r + 128]).astype(BF16)
            for r in range(i * width, (i + 1) * width, 128)
        ]
        scaled = jnp.concatenate(scaled, axis=1)
        copies[i][1].wait()
        copies[i][2].wait()
        term = lax.dot_general(
            scaled,
            frames_both[:, i * width : (i + 1) * width],
            (((1,), (1,)), ((), ())),
            preferred_element_type=F32,
        )
        total[...] = term if i == 0 else total[...] + term
    count = len(piece_refs)
    size = columns // count
    for k, piece_ref in enumerate(piece_refs):
        at = pl.multiple_of(lax.rem(me_ref[0] + k, count) * size, size)
        piece_ref[...] = total[pl.ds(at, size), :].astype(piece_ref.dtype)


def project(me, count, frames_now, frames_lag, test_matrix, scale):
    frames, features = frames_now.shape
    columns = test_matrix.shape[1]
    parts = 4
    size = columns // count
    vmem = pl.BlockSpec(memory_space=pltpu.VMEM)
    hbm = pl.BlockSpec(memory_space=pl.ANY)
    return pl.pallas_call(
        lambda *refs: project_kernel(parts, *refs),
        in_specs=[pl.BlockSpec(memory_space=pltpu.SMEM), hbm, hbm, hbm, hbm],
        out_specs=[vmem] * count,
        out_shape=[jax.ShapeDtypeStruct((size, 2 * frames), F32)]
        + [jax.ShapeDtypeStruct((size, 2 * frames), BF16)] * (count - 1),
        scratch_shapes=[
            pltpu.VMEM((2 * frames, features), BF16),
            pltpu.VMEM((features, columns), BF16),
            pltpu.VMEM((1, features), F32),
            pltpu.VMEM((columns, 2 * frames), F32),
            pltpu.SemaphoreType.DMA((3 * parts + 1,)),
        ],
        compiler_params=pltpu.CompilerParams(vmem_limit_bytes=32 * 2**20),
        cost_estimate=pl.CostEstimate(
            flops=4 * frames * features * columns, bytes_accessed=4 * frames * features, transcendentals=0
        ),
        name="project",
    )(me[None], in_hbm(frames_now), in_hbm(frames_lag), in_hbm(test_matrix), in_hbm(scale))


def cross_kernel(jobs, where_ref, proj_ref, now_hbm, lag_hbm, factor_ref, *refs):
    *out_refs, work, sems = refs
    frames = now_hbm.shape[0]
    block = out_refs[0].shape[2]
    count = now_hbm.shape[1] // (2 * block)
    places = []
    copies = []
    for n, (_, _, other, slot) in enumerate(jobs):
        half = 1 - where_ref[0] if other else where_ref[0]
        first = half * count + lax.rem(where_ref[1] + slot, count)
        at = pl.ds(pl.multiple_of(first * block, block), block)
        places.append(at)
        copies.append(
            [
                pltpu.make_async_copy(now_hbm.at[:, at], work.at[n, pl.ds(0, frames)], sems.at[2 * n]),
                pltpu.make_async_copy(lag_hbm.at[:, at], work.at[n, pl.ds(frames, frames)], sems.at[2 * n + 1]),
            ]
        )
        for copy in copies[-1]:
            copy.start()
    proj = jnp.concatenate([proj_ref[:, frames:], proj_ref[:, :frames]], axis=1)
    for n, (out, row, _, _) in enumerate(jobs):
        for copy in copies[n]:
            copy.wait()
        total = jnp.dot(proj, work[n], preferred_element_type=F32)
        out_refs[out][row] = (total * factor_ref[:, places[n]]).astype(out_refs[out].dtype)


def cross(core, ring_place, ring, slots_other, slots_own, proj, frames_now, frames_lag, factor):
    frames, features = frames_now.shape
    columns = proj.shape[0]
    block = features // (2 * ring)
    jobs, out_shape = [], []
    for slots, other, dtype in ((slots_other, True, BF16), (slots_own, False, F32)):
        if slots:
            jobs += [(len(out_shape), row, other, slot) for row, slot in enumerate(slots)]
            out_shape.append(jax.ShapeDtypeStruct((len(slots), columns, block), dtype))
    vmem = pl.BlockSpec(memory_space=pltpu.VMEM)
    hbm = pl.BlockSpec(memory_space=pl.ANY)
    return pl.pallas_call(
        lambda *refs: cross_kernel(jobs, *refs),
        in_specs=[pl.BlockSpec(memory_space=pltpu.SMEM), vmem, hbm, hbm, vmem],
        out_specs=[vmem] * len(out_shape),
        out_shape=out_shape,
        scratch_shapes=[
            pltpu.VMEM((len(jobs), 2 * frames, block), BF16),
            pltpu.SemaphoreType.DMA((2 * len(jobs),)),
        ],
        compiler_params=pltpu.CompilerParams(vmem_limit_bytes=24 * 2**20),
        cost_estimate=pl.CostEstimate(
            flops=4 * frames * len(jobs) * block * columns,
            bytes_accessed=4 * frames * len(jobs) * block,
            transcendentals=0,
        ),
        name="cross",
    )(jnp.stack([core, ring_place]), proj, in_hbm(frames_now), in_hbm(frames_lag), factor)


def combine_kernel(own_ref, came_ref, *out_refs):
    for k, out_ref in enumerate(out_refs):
        out_ref[...] = (own_ref[k] + came_ref[k].astype(F32)).astype(BF16)


def combine(own, came, count):
    _, columns, block = own.shape
    whole = pl.BlockSpec(memory_space=pltpu.VMEM)
    return pl.pallas_call(
        combine_kernel,
        in_specs=[whole] * 2,
        out_specs=[whole] * count,
        out_shape=[jax.ShapeDtypeStruct((columns, block), BF16)] * count,
        compiler_params=pltpu.CompilerParams(vmem_limit_bytes=16 * 2**20),
        name="combine",
    )(own, came)


def gram_kernel(own_ref, came_ref, a_ref, b_ref, d_ref, gram_ref, rows_ref):
    last = own_ref.shape[0] - 1
    total = own_ref[last] + came_ref[last].astype(F32)
    total = total + (a_ref[...].astype(F32) + b_ref[...].astype(F32) + d_ref[...].astype(F32))
    gram_ref[...] = lax.dot_general(
        total, total, (((1,), (1,)), ((), ())), precision=EXACT, preferred_element_type=F32
    )
    rows_ref[...] = jnp.transpose(total).astype(BF16)


def gram_of(own, came, others):
    columns, block = own.shape[1:]
    whole = pl.BlockSpec(memory_space=pltpu.VMEM)
    return pl.pallas_call(
        gram_kernel,
        in_specs=[whole] * 5,
        out_specs=[whole] * 2,
        out_shape=[
            jax.ShapeDtypeStruct((columns, columns), F32),
            jax.ShapeDtypeStruct((block, columns), BF16),
        ],
        compiler_params=pltpu.CompilerParams(vmem_limit_bytes=16 * 2**20),
        name="gram",
    )(own, came, *others)


def basis_kernel(parts, core_ref, first_ref, second_ref, high_ref, low_ref, out_hbm, work, sems):
    transposed = (((1,), (1,)), ((), ()))
    size = work.shape[0] // parts
    copies = []
    for i in range(parts):
        at = slice(i * size, (i + 1) * size)
        sketch = jnp.where(core_ref[0] == 0, first_ref[at, :], second_ref[at, :])
        total = lax.dot_general(sketch, high_ref[...], transposed, preferred_element_type=F32)
        total = total + lax.dot_general(sketch, low_ref[...], transposed, preferred_element_type=F32)
        work[at, :] = total.astype(BF16)
        rows = pl.ds(i * size, size)
        copies.append(pltpu.make_async_copy(work.at[rows], out_hbm.at[rows], sems.at[i]))
        copies[-1].start()
    for copy in copies:
        copy.wait()


def basis_of(core, first, second, high, low):
    rows, columns = first.shape
    parts = 8
    vmem = pl.BlockSpec(memory_space=pltpu.VMEM)
    return pl.pallas_call(
        lambda *refs: basis_kernel(parts, *refs),
        in_specs=[pl.BlockSpec(memory_space=pltpu.SMEM)] + [vmem] * 4,
        out_specs=pl.BlockSpec(memory_space=pl.ANY),
        out_shape=jax.ShapeDtypeStruct((rows, columns), BF16),
        scratch_shapes=[pltpu.VMEM((rows, columns), BF16), pltpu.SemaphoreType.DMA((parts,))],
        compiler_params=pltpu.CompilerParams(vmem_limit_bytes=16 * 2**20),
        cost_estimate=pl.CostEstimate(
            flops=4 * rows * columns * columns, bytes_accessed=4 * rows * columns, transcendentals=0
        ),
        name="basis",
    )(core[None], first, second, high, low)


def on_device(frames_now, frames_lag, test_matrix, feature_scale):
    frames, features = frames_now.shape
    frame_total = frames * lax.axis_size(("y", "c"))
    feature_total = features * lax.axis_size(("z", "x"))
    ring = lax.axis_size("y")
    scale = feature_scale[None, :]
    factor = (0.5 / frame_total) * scale
    with jax.named_scope("project"):
        own, *pieces = project(
            lax.axis_index("x"), lax.axis_size("x"), frames_now, frames_lag, test_matrix, scale
        )
        for k in (2, 1, 3):
            own = own + shifted(pieces[k - 1], "x", -k).astype(F32)
        proj = gather(ring_sum(own, "z").astype(BF16), "x")

    with jax.named_scope("sketch"):
        y = lax.axis_index("y")
        c = lax.axis_index("c")
        terms = (frames_now, frames_lag, factor)
        send, own = cross(c, y, ring, (2,), (2,), proj, *terms)
        send, proj = lax.optimization_barrier((send, proj))
        came = swapped(send, "c", 1)
        (send,) = cross(c, y, ring, (1, 3, 0), (), proj, *terms)
        (piece,) = combine(own, came, 1)
        send, proj, piece = lax.optimization_barrier((send, proj, piece))
        others = [shifted(piece, "y", -2)]
        came = swapped(send, "c", 1)
        (own,) = cross(c, y, ring, (), (1, 3, 0), proj, *terms)
        pieces = combine(own, came, 2)
        others += [shifted(pieces[0], "y", -1), shifted(pieces[1], "y", -3)]

    with jax.named_scope("gram"):
        partial, mine = gram_of(own, came, others)
        slab = partial + lax.ppermute(partial, "c", [(0, 1)])
        pair = jnp.stack([mine, lax.ppermute(mine, "c", [(1, 0)])])
        slab = scatter_sum(slab, "x", 1)
        slab = exact_sum(slab, "z", (1, 6, 7), 1)
        slab = exact_sum(slab, "z", (2,), 1)
        slab = exact_sum(slab, "y", (1, 2, 3), 1)
        gram = gather(slab, "x", 1)
        whole = gather(pair, "y", 0, 1).reshape(features, -1)
        gram = jnp.where(c == 1, gram, lax.ppermute(gram, "c", [(1, 0)]))
        gram, whole = lax.optimization_barrier((gram, whole))
        copied = lax.ppermute(whole, "c", [(0, 1)])
        upper, high, low = factorize(gram, feature_total**0.5)
    return (basis_of(c, whole, copied, high, low), upper)


def solution(mesh):
    split = Mesh(mesh.devices.reshape(4, 2, 8, 4), ("y", "c", "z", "x"))
    traj, feat = ("y", "c"), ("z", "x")
    in_specs = (P(traj, feat), P(traj, feat), P(feat, None), P(feat))
    out_specs = (P(feat, None), P())
    return jax.shard_map(
        on_device, mesh=split, in_specs=in_specs, out_specs=out_specs, check_vma=False
    )
```

```python
import jax
import jax.numpy as jnp
from jax import lax
from jax.experimental import pallas as pl
from jax.experimental.pallas import tpu as pltpu
from jax.sharding import Mesh
from jax.sharding import PartitionSpec as P

F32 = jnp.float32
BF16 = jnp.bfloat16
EXACT = lax.Precision.HIGHEST


def moved(x, axis, source, mixed):
    n = lax.axis_size(axis)
    if not mixed:
        return lax.ppermute(x, axis, [(source(i, n), i) for i in range(n)])
    pairs = []
    for i in range(n):
        for c in range(2):
            j = source(i, n)
            d = c ^ ((i + j) % 2)
            pairs.append((2 * j + d, 2 * i + c) if axis == "y" else (d * n + j, c * n + i))
    return lax.ppermute(x, (axis, "c") if axis == "y" else ("c", axis), pairs)


def shifted(x, axis, by, mixed=False):
    return moved(x, axis, lambda i, n: (i + by) % n, mixed)


def swapped(x, axis, mask, mixed=False):
    return moved(x, axis, lambda i, n: i ^ mask, mixed)


def piece(x, index, size):
    return lax.dynamic_slice_in_dim(x, index * size, size, axis=0)


def scatter_sum(x, axis, mixed):
    n = lax.axis_size(axis)
    me = lax.axis_index(axis)
    size = x.shape[0] // n
    total = piece(x, me, size)
    for by in (2, 1, 3):
        total = total + shifted(piece(x, (me + by) % n, size), axis, n - by, mixed)
    return total


def placed(pieces, axis):
    n = len(pieces)
    me = lax.axis_index(axis)
    size = pieces[0].shape[0]
    out = jnp.zeros((n * size, pieces[0].shape[1]), pieces[0].dtype)
    for k, piece_k in enumerate(pieces):
        out = lax.dynamic_update_slice_in_dim(out, piece_k, ((me + k) % n) * size, axis=0)
    return out


def gather(x, axis, mixed=False):
    came = {k: shifted(x, axis, k, mixed) for k in (2, 1, 3)}
    return placed([x] + [came[k] for k in (1, 2, 3)], axis)


def gather_cores(x, place):
    other = swapped(x, "c", 1)
    size = x.shape[0]
    out = jnp.zeros((2 * size, x.shape[1]), x.dtype)
    out = lax.dynamic_update_slice_in_dim(out, x, place * size, axis=0)
    return lax.dynamic_update_slice_in_dim(out, other, (1 - place) * size, axis=0)


def ring_sum(x, axis):
    own = x.astype(BF16)
    before = shifted(own, axis, -1).astype(F32)
    after = shifted(own, axis, 1).astype(F32)
    two = x + before
    three = two + after
    far = shifted(three.astype(BF16), axis, 3).astype(F32)
    near = shifted(two.astype(BF16), axis, -2).astype(F32)
    return three + (far + near)


def exact_sum(x, axis, masks):
    came = [swapped(x, axis, mask, True) for mask in masks]
    return x + came[0] if len(came) == 1 else (x + came[0]) + (came[1] + came[2])


def factor_block(tile, lead, size):
    groups = size // 8
    rows = [tile[8 * g : 8 * g + 8, :] for g in range(groups)]
    sub = lax.broadcasted_iota(jnp.int32, (8, 128), 0)
    for q in range(groups):
        first = lead + 8 * q
        column = [
            [jnp.broadcast_to(rows[g][:, first + k : first + k + 1], (8, 128)) for g in range(q, groups)]
            for k in range(8)
        ]
        pivots = jnp.zeros((8, 128), F32)
        for j in range(8):
            pivot = jnp.broadcast_to(column[j][0][j : j + 1, :], (8, 128))
            inverse = 1.0 / pivot
            pivots = jnp.where(sub == j, pivot, pivots)
            factor = [c * inverse for c in column[j]]
            factor[0] = jnp.where(sub > j, factor[0], 0.0)
            for k in range(j + 1, 8):
                top = jnp.broadcast_to(column[k][0][j : j + 1, :], (8, 128))
                column[k] = [c - f * top for c, f in zip(column[k], factor)]
            top = jnp.broadcast_to(rows[q][j : j + 1, :], (8, 128))
            for g in range(q, groups):
                rows[g] = rows[g] - factor[g - q] * top
        rows[q] = rows[q] * lax.rsqrt(pivots)
    return jnp.concatenate(rows, axis=0)


def factor_kernel(scale, gram_ref, upper_ref, high_ref, low_ref, work):
    n = gram_ref.shape[0]
    size = 64
    row = lax.broadcasted_iota(jnp.int32, (n, n), 0)
    col = lax.broadcasted_iota(jnp.int32, (n, n), 1)
    work[:, :n] = gram_ref[...]
    work[:, n:] = jnp.where(row == col, 1.0, 0.0).astype(F32)
    block_row = lax.broadcasted_iota(jnp.int32, (size, 128), 0)
    block_col = lax.broadcasted_iota(jnp.int32, (size, 128), 1)
    for r0 in range(0, n, size):
        r1 = r0 + size
        lead = r0 % 128
        other = (lead + size) % 128
        tile = work[r0:r1, r0 - lead : r0 - lead + 128]
        mine = (block_col >= lead) & (block_col < lead + size)
        tile = jnp.where(mine, tile, jnp.where(block_col - other == block_row, 1.0, 0.0))
        tile = factor_block(tile, lead, size)
        inverse = tile[:, other : other + size]
        panel = jnp.dot(inverse, work[r0:r1, :], precision=EXACT, preferred_element_type=F32)
        work[r0:r1, :] = panel
        if r1 < n:
            work[r1:, :] = work[r1:, :] - lax.dot_general(
                panel[:, r1:n], panel, (((0,), (0,)), ((), ())), precision=EXACT, preferred_element_type=F32
            )
    upper_ref[...] = jnp.where(row <= col, work[:, :n], 0.0)
    inverse = jnp.where(row >= col, work[:, n:], 0.0) * scale
    high = inverse.astype(BF16)
    high_ref[...] = high
    low_ref[...] = (inverse - high.astype(F32)).astype(BF16)


def factorize(gram, scale):
    n = gram.shape[0]
    whole = pl.BlockSpec(memory_space=pltpu.VMEM)
    return pl.pallas_call(
        lambda *refs: factor_kernel(scale, *refs),
        out_shape=[
            jax.ShapeDtypeStruct((n, n), F32),
            jax.ShapeDtypeStruct((n, n), BF16),
            jax.ShapeDtypeStruct((n, n), BF16),
        ],
        in_specs=[whole],
        out_specs=[whole] * 3,
        scratch_shapes=[pltpu.VMEM((n, 2 * n), F32)],
        compiler_params=pltpu.CompilerParams(vmem_limit_bytes=16 * 2**20),
        cost_estimate=pl.CostEstimate(flops=12 * n * n * n, bytes_accessed=8 * n * n, transcendentals=0),
        name="factorize",
    )(gram)


def in_hbm(x):
    return pltpu.with_memory_space_constraint(x, pltpu.HBM)


def project_kernel(parts, me_ref, now_hbm, lag_hbm, test_hbm, scale_hbm, *refs):
    *piece_refs, frames_both, test, scale_ref, total, sems = refs
    frames, features = now_hbm.shape
    columns = test.shape[1]
    width = features // parts
    copies = []
    scales = pltpu.make_async_copy(scale_hbm, scale_ref, sems.at[3 * parts])
    scales.start()
    for i in range(parts):
        at = pl.ds(i * width, width)
        copies.append(
            [
                pltpu.make_async_copy(test_hbm.at[at], test.at[at], sems.at[3 * i]),
                pltpu.make_async_copy(now_hbm.at[:, at], frames_both.at[pl.ds(0, frames), at], sems.at[3 * i + 1]),
                pltpu.make_async_copy(lag_hbm.at[:, at], frames_both.at[pl.ds(frames, frames), at], sems.at[3 * i + 2]),
            ]
        )
        for copy in copies[-1]:
            copy.start()
    scales.wait()
    for i in range(parts):
        copies[i][0].wait()
        scaled = [
            (jnp.transpose(test[r : r + 128, :]).astype(F32) * scale_ref[:, r : r + 128]).astype(BF16)
            for r in range(i * width, (i + 1) * width, 128)
        ]
        scaled = jnp.concatenate(scaled, axis=1)
        copies[i][1].wait()
        copies[i][2].wait()
        term = lax.dot_general(
            scaled,
            frames_both[:, i * width : (i + 1) * width],
            (((1,), (1,)), ((), ())),
            preferred_element_type=F32,
        )
        total[...] = term if i == 0 else total[...] + term
    count = len(piece_refs)
    size = columns // count
    for k, piece_ref in enumerate(piece_refs):
        at = pl.multiple_of(lax.rem(me_ref[0] + k, count) * size, size)
        piece_ref[...] = total[pl.ds(at, size), :].astype(piece_ref.dtype)


def project(me, count, frames_now, frames_lag, test_matrix, scale):
    frames, features = frames_now.shape
    columns = test_matrix.shape[1]
    parts = 4
    size = columns // count
    vmem = pl.BlockSpec(memory_space=pltpu.VMEM)
    hbm = pl.BlockSpec(memory_space=pl.ANY)
    return pl.pallas_call(
        lambda *refs: project_kernel(parts, *refs),
        in_specs=[pl.BlockSpec(memory_space=pltpu.SMEM), hbm, hbm, hbm, hbm],
        out_specs=[vmem] * count,
        out_shape=[jax.ShapeDtypeStruct((size, 2 * frames), F32)]
        + [jax.ShapeDtypeStruct((size, 2 * frames), BF16)] * (count - 1),
        scratch_shapes=[
            pltpu.VMEM((2 * frames, features), BF16),
            pltpu.VMEM((features, columns), BF16),
            pltpu.VMEM((1, features), F32),
            pltpu.VMEM((columns, 2 * frames), F32),
            pltpu.SemaphoreType.DMA((3 * parts + 1,)),
        ],
        compiler_params=pltpu.CompilerParams(vmem_limit_bytes=32 * 2**20),
        cost_estimate=pl.CostEstimate(
            flops=4 * frames * features * columns, bytes_accessed=4 * frames * features, transcendentals=0
        ),
        name="project",
    )(me[None], in_hbm(frames_now), in_hbm(frames_lag), in_hbm(test_matrix), in_hbm(scale))


def cross_kernel(jobs, where_ref, proj_ref, now_hbm, lag_hbm, factor_ref, *refs):
    *out_refs, work, sems = refs
    frames = now_hbm.shape[0]
    block = out_refs[0].shape[2]
    count = now_hbm.shape[1] // (2 * block)
    places = []
    copies = []
    for n, (_, _, other, slot) in enumerate(jobs):
        half = 1 - where_ref[0] if other else where_ref[0]
        first = half * count + lax.rem(where_ref[1] + slot, count)
        at = pl.ds(pl.multiple_of(first * block, block), block)
        places.append(at)
        copies.append(
            [
                pltpu.make_async_copy(now_hbm.at[:, at], work.at[n, pl.ds(0, frames)], sems.at[2 * n]),
                pltpu.make_async_copy(lag_hbm.at[:, at], work.at[n, pl.ds(frames, frames)], sems.at[2 * n + 1]),
            ]
        )
        for copy in copies[-1]:
            copy.start()
    proj = jnp.concatenate([proj_ref[:, frames:], proj_ref[:, :frames]], axis=1)
    for n, (out, row, _, _) in enumerate(jobs):
        for copy in copies[n]:
            copy.wait()
        total = jnp.dot(proj, work[n], preferred_element_type=F32)
        out_refs[out][row] = (total * factor_ref[:, places[n]]).astype(out_refs[out].dtype)


def cross(core, ring_place, ring, slots_other, slots_own, proj, frames_now, frames_lag, factor):
    frames, features = frames_now.shape
    columns = proj.shape[0]
    block = features // (2 * ring)
    jobs, out_shape = [], []
    for slots, other, dtype in ((slots_other, True, BF16), (slots_own, False, F32)):
        if slots:
            jobs += [(len(out_shape), row, other, slot) for row, slot in enumerate(slots)]
            out_shape.append(jax.ShapeDtypeStruct((len(slots), columns, block), dtype))
    vmem = pl.BlockSpec(memory_space=pltpu.VMEM)
    hbm = pl.BlockSpec(memory_space=pl.ANY)
    return pl.pallas_call(
        lambda *refs: cross_kernel(jobs, *refs),
        in_specs=[pl.BlockSpec(memory_space=pltpu.SMEM), vmem, hbm, hbm, vmem],
        out_specs=[vmem] * len(out_shape),
        out_shape=out_shape,
        scratch_shapes=[
            pltpu.VMEM((len(jobs), 2 * frames, block), BF16),
            pltpu.SemaphoreType.DMA((2 * len(jobs),)),
        ],
        compiler_params=pltpu.CompilerParams(vmem_limit_bytes=24 * 2**20),
        cost_estimate=pl.CostEstimate(
            flops=4 * frames * len(jobs) * block * columns,
            bytes_accessed=4 * frames * len(jobs) * block,
            transcendentals=0,
        ),
        name="cross",
    )(jnp.stack([core, ring_place]), proj, in_hbm(frames_now), in_hbm(frames_lag), factor)


def combine_kernel(own_ref, came_ref, *out_refs):
    for k, out_ref in enumerate(out_refs):
        out_ref[...] = (own_ref[k] + came_ref[k].astype(F32)).astype(BF16)


def combine(own, came, count):
    _, columns, block = own.shape
    whole = pl.BlockSpec(memory_space=pltpu.VMEM)
    return pl.pallas_call(
        combine_kernel,
        in_specs=[whole] * 2,
        out_specs=[whole] * count,
        out_shape=[jax.ShapeDtypeStruct((columns, block), BF16)] * count,
        compiler_params=pltpu.CompilerParams(vmem_limit_bytes=16 * 2**20),
        name="combine",
    )(own, came)


def gram_kernel(side_ref, own_ref, came_ref, a_ref, b_ref, d_ref, keep_ref, send_ref, rows_ref, work):
    total = own_ref[own_ref.shape[0] - 1] + came_ref[own_ref.shape[0] - 1].astype(F32)
    total = total + (a_ref[...].astype(F32) + b_ref[...].astype(F32) + d_ref[...].astype(F32))
    half = keep_ref.shape[0]
    side = side_ref[0]
    work[...] = lax.dot_general(
        total, total, (((1,), (1,)), ((), ())), precision=EXACT, preferred_element_type=F32
    )
    keep_ref[...] = work[pl.ds(pl.multiple_of(side * half, half), half), :]
    send_ref[...] = work[pl.ds(pl.multiple_of((1 - side) * half, half), half), :]
    rows_ref[...] = jnp.transpose(total).astype(BF16)


def gram_of(side, own, came, others):
    columns, block = own.shape[1:]
    whole = pl.BlockSpec(memory_space=pltpu.VMEM)
    half = jax.ShapeDtypeStruct((columns // 2, columns), F32)
    return pl.pallas_call(
        gram_kernel,
        in_specs=[pl.BlockSpec(memory_space=pltpu.SMEM)] + [whole] * 5,
        out_specs=[whole] * 3,
        out_shape=[half, half, jax.ShapeDtypeStruct((block, columns), BF16)],
        scratch_shapes=[pltpu.VMEM((columns, columns), F32)],
        compiler_params=pltpu.CompilerParams(vmem_limit_bytes=16 * 2**20),
        name="gram",
    )(side, own, came, *others)


def basis_kernel(parts, sketch_ref, high_ref, low_ref, out_hbm, work, sems):
    transposed = (((1,), (1,)), ((), ()))
    size = work.shape[0] // parts
    copies = []
    for i in range(parts):
        at = slice(i * size, (i + 1) * size)
        total = lax.dot_general(sketch_ref[at, :], high_ref[...], transposed, preferred_element_type=F32)
        total = total + lax.dot_general(sketch_ref[at, :], low_ref[...], transposed, preferred_element_type=F32)
        work[at, :] = total.astype(BF16)
        rows = pl.ds(i * size, size)
        copies.append(pltpu.make_async_copy(work.at[rows], out_hbm.at[rows], sems.at[i]))
        copies[-1].start()
    for copy in copies:
        copy.wait()


def basis_of(sketch, high, low):
    rows, columns = sketch.shape
    parts = 8
    vmem = pl.BlockSpec(memory_space=pltpu.VMEM)
    return pl.pallas_call(
        lambda *refs: basis_kernel(parts, *refs),
        in_specs=[vmem] * 3,
        out_specs=pl.BlockSpec(memory_space=pl.ANY),
        out_shape=jax.ShapeDtypeStruct((rows, columns), BF16),
        scratch_shapes=[pltpu.VMEM((rows, columns), BF16), pltpu.SemaphoreType.DMA((parts,))],
        compiler_params=pltpu.CompilerParams(vmem_limit_bytes=16 * 2**20),
        cost_estimate=pl.CostEstimate(
            flops=4 * rows * columns * columns, bytes_accessed=4 * rows * columns, transcendentals=0
        ),
        name="basis",
    )(sketch, high, low)


def on_device(frames_now, frames_lag, test_matrix, feature_scale):
    frames, features = frames_now.shape
    frame_total = frames * lax.axis_size(("y", "c"))
    feature_total = features * lax.axis_size(("z", "x"))
    ring = lax.axis_size("y")
    scale = feature_scale[None, :]
    factor = (0.5 / frame_total) * scale
    with jax.named_scope("project"):
        own, *pieces = project(
            lax.axis_index("x"), lax.axis_size("x"), frames_now, frames_lag, test_matrix, scale
        )
        for k in (2, 1, 3):
            own = own + shifted(pieces[k - 1], "x", -k).astype(F32)
        proj = gather(ring_sum(own, "z").astype(BF16), "x")

    with jax.named_scope("sketch"):
        y = lax.axis_index("y")
        c = lax.axis_index("c")
        terms = (frames_now, frames_lag, factor)
        send, own = cross(c, y, ring, (2,), (2,), proj, *terms)
        send, proj = lax.optimization_barrier((send, proj))
        came = swapped(send, "c", 1)
        (send,) = cross(c, y, ring, (1, 3, 0), (), proj, *terms)
        (piece,) = combine(own, came, 1)
        send, proj, piece = lax.optimization_barrier((send, proj, piece))
        others = [shifted(piece, "y", -2)]
        came = swapped(send, "c", 1)
        (own,) = cross(c, y, ring, (), (1, 3, 0), proj, *terms)
        pieces = combine(own, came, 2)
        others += [shifted(pieces[0], "y", -1), shifted(pieces[1], "y", -3)]

    with jax.named_scope("gram"):
        side = (c + lax.axis_index("x") + y + lax.axis_index("z")) % 2
        keep, send, mine = gram_of(side[None], own, came, others)
        slab = keep + swapped(send, "c", 1)
        slab, mine = lax.optimization_barrier((slab, mine))
        across = shifted(mine, "y", 2)
        slab = scatter_sum(slab, "x", True)
        slab, across = lax.optimization_barrier((slab, across))
        ahead, behind = shifted(mine, "y", 1), shifted(mine, "y", -1)
        slab = exact_sum(slab, "z", (1, 6, 7))
        slab = exact_sum(slab, "z", (2,))
        slab, ahead, behind = lax.optimization_barrier((slab, ahead, behind))
        slab = exact_sum(slab, "y", (1, 2, 3))
        gram = gather_cores(gather(slab, "x", True), side)
        whole = placed((mine, ahead, across, behind), "y")
        gram, whole = lax.optimization_barrier((gram, whole))
        whole = gather_cores(whole, c)
        upper, high, low = factorize(gram, feature_total**0.5)
    return (basis_of(whole, high, low), upper)


def solution(mesh):
    split = Mesh(mesh.devices.reshape(4, 2, 8, 4), ("y", "c", "z", "x"))
    traj, feat = ("y", "c"), ("z", "x")
    in_specs = (P(traj, feat), P(traj, feat), P(feat, None), P(feat))
    out_specs = (P(feat, None), P())
    return jax.shard_map(
        on_device, mesh=split, in_specs=in_specs, out_specs=out_specs, check_vma=False
    )
```
